256 devices in a mesh: segment: 16 (over x_hi, y, core), expert: 16 (over x_lo, z).
Axes of the slice: x: 4 (x_hi: 2, x_lo: 2; x = x_hi * 2 + x_lo), y: 4, z: 8, core: 2. Of those that a mesh axis runs over, the one named last changes fastest.
Arguments:
- fwd_tokens: bfloat16 [16, 2048, 2048], P('segment', 'expert'), may hold values from -6 to 6
- fwd_routes: int32 [16, 2048, 2], P('segment', 'expert'), may hold values from 0 to 15, all different within a row; in each aligned block of 128 rows (0 to 127, 128 to 255, ..., all dimensions but the last counted through in order) at most 32 rows name the same one
- fwd_weights: float32 [16, 2048, 2], P('segment', 'expert'), may hold values from 0.2 to 1
- saved_tokens: bfloat16 [16, 2048, 2048], P('segment', 'expert'), may hold values from -6 to 6
- bwd_routes: int32 [16, 2048, 2], P('segment', 'expert'), may hold values from 0 to 15, all different within a row; in each aligned block of 128 rows (0 to 127, 128 to 255, ..., all dimensions but the last counted through in order) at most 32 rows name the same one
- bwd_weights: float32 [16, 2048, 2], P('segment', 'expert'), may hold values from 0.2 to 1
- incoming_grad: bfloat16 [16, 2048, 2048], P('segment', 'expert'), may hold values from -6 to 6
- norm_gain: float32 [16, 2048], P('segment'), may hold values from 0.1 to 1.9
- gate_proj: bfloat16 [16, 16, 2048, 768], P('segment', 'expert'), may hold values from -0.125 to 0.125
- up_proj: bfloat16 [16, 16, 2048, 768], P('segment', 'expert'), may hold values from -0.125 to 0.125
- down_proj: bfloat16 [16, 16, 768, 2048], P('segment', 'expert'), may hold values from -0.21875 to 0.21875
Outputs:
- next_input: bfloat16 [16, 2048, 2048], P('segment', 'expert')
- next_grad: bfloat16 [16, 2048, 2048], P('segment', 'expert')
- combine_grad: bfloat16 [16, 2048, 2], P('segment', 'expert')
The draws below stay inside these ranges and needn't reach their ends.
Inputs may be any that keep to these rules, and one draw needn't show every extreme that they name: `fwd_routes`: each token names 2 different experts. In each aligned block of 128 rows of a section (the rows of one device), no expert is named more than 32 times, and in every draw some expert is named exactly 32 times in some block. `bwd_routes`: as for fwd_routes.
All inputs are finite; a program needn't handle non-finite values.
Results may differ from the reference program's by a relative error of at most 0.012.
Values may be sent and summed in bfloat16 or wider, within the bound.
A program may use at most 128 MiB of HBM per device.

```python
import math
from functools import partial
import jax
import jax.numpy as jnp
import numpy as np
from jax import lax

D = 2048
FF = 768
TOPK = 2
TOK_DEV = 128
EXPERTS = 16
TOKENS = 2048
SECTIONS = 16
CAP = 32
N_EXPERT = 16


def levels(key, extent, shards, low, high):
    level = 1.0
    for axis_at, parts in shards:
        steps = jax.random.uniform(jax.random.fold_in(jax.random.fold_in(key, 6), axis_at), (parts,), jnp.float32, low / len(shards), high / len(shards))
        level = level * jnp.repeat(jnp.exp(steps), extent[axis_at] // parts).reshape((-1,) + (1,) * (len(extent) - 1 - axis_at))
    return level


def deal_out(own_key, own, number, rows, count, top, limit, skew):
    sequence = jax.random.permutation(own_key, count)
    crowded, ordinary = portions_of(count, rows * top, limit, skew, True), portions_of(count, rows * top, limit, skew, False)
    places = jnp.arange(count)

    def named(tallies, offset_by):
        used = int((tallies > 0).sum())
        fixed = max(1, used // 4)
        shifted = fixed + (places - fixed + offset_by * (used - fixed)) % max(1, count - fixed)
        return jnp.zeros((count,), jnp.int32).at[sequence[jnp.where(places < fixed, places, shifted)]].set(jnp.asarray(tallies, jnp.int32))

    tallies = jnp.where(number % 4 == 0, named(crowded, number // 4), named(ordinary, number - number // 4 - 1))
    mixed = jax.random.permutation(jax.random.fold_in(own, 3), count)
    source_of, taker = mixed[0:count // 2 * 2:2], mixed[1:count // 2 * 2:2]
    room = jnp.minimum(tallies[source_of] - 1, limit - tallies[taker]) // 2
    room = jnp.where((source_of == sequence[0]) | (taker == sequence[0]) | (tallies[taker] == 0), 0, jnp.maximum(room, 0))
    shifted = jax.random.randint(jax.random.fold_in(own, 4), (count // 2,), 0, 1 << 20) % (room + 1)
    tallies = tallies.at[source_of].add(-shifted).at[taker].add(shifted)
    members = jnp.searchsorted(jnp.cumsum(tallies), jnp.arange(rows * top), side="right").astype(jnp.int32)
    table = members.reshape(top, rows).T
    table = table[jax.random.permutation(jax.random.fold_in(own, 1), rows)]
    offset_by = jax.random.randint(jax.random.fold_in(own, 2), (rows, 1), 0, top)
    return jnp.take_along_axis(table, (jnp.arange(top)[None, :] + offset_by) % top, axis=1)


def portions_of(count, total, most, lean, full):
    weights = [(1 << 20) // math.isqrt(rank ** lean) + 1 for rank in range(1, count + 1)]
    largest = most if full else min(most, max(-(-total // count), total * weights[0] // sum(weights)))
    least = 1 if total - largest >= count - 1 else 0
    given, rest = [largest] + [least] * (count - 1), total - largest - least * (count - 1)
    while rest > 0:
        movable = [i for i in range(1, count) if given[i] < largest] or [i for i in range(1, count) if given[i] < most]
        pool, left = sum([weights[i] for i in movable]), rest
        for i in movable:
            extra = min(most - given[i], max(1, left * weights[i] // pool), rest)
            given[i] = given[i] + extra
            rest = rest - extra
    return np.array(given)


def gaussian(key, shape, width, bound, split=(), kind=jnp.bfloat16):
    result = width * jax.random.normal(key, shape, jnp.float32)
    if split:
        result = result * levels(key, shape, split, -0.22, 0.18)
    return jnp.clip(result, -bound, bound).astype(kind)


def setup_inputs(seed: int = 0) -> dict:
    splits = jax.random.split(jax.random.key(seed), 12)
    fwd_tokens = gaussian(splits[0], (SECTIONS, TOKENS, D), 1.0, 6.0, ((0, 16), (1, 16)))
    fwd_routes_keys = jax.random.split(jax.random.fold_in(splits[1], 1), SECTIONS * TOKENS // TOK_DEV)
    fwd_routes_turns = jax.random.permutation(jax.random.fold_in(splits[1], 3), SECTIONS * TOKENS // TOK_DEV)
    fwd_routes = jax.vmap(lambda own, number: deal_out(jax.random.fold_in(splits[1], 2), own, number, TOK_DEV, EXPERTS, TOPK, CAP, 2))(fwd_routes_keys, fwd_routes_turns).reshape((SECTIONS, TOKENS, TOPK))
    fwd_weights = jnp.clip(jnp.exp(math.log(1.0) - 1.609438 * jax.random.uniform(splits[2], (SECTIONS, TOKENS, TOPK), jnp.float32) ** levels(splits[2], (SECTIONS, TOKENS, TOPK), ((0, 16), (1, 16)), -0.2, 0.2)), 0.2, 1.0)
    saved_tokens = gaussian(splits[3], (SECTIONS, TOKENS, D), 1.0, 6.0, ((0, 16), (1, 16)))
    bwd_routes_keys = jax.random.split(jax.random.fold_in(splits[4], 1), SECTIONS * TOKENS // TOK_DEV)
    bwd_routes_turns = jax.random.permutation(jax.random.fold_in(splits[4], 3), SECTIONS * TOKENS // TOK_DEV)
    bwd_routes = jax.vmap(lambda own, number: deal_out(jax.random.fold_in(splits[4], 2), own, number, TOK_DEV, EXPERTS, TOPK, CAP, 2))(bwd_routes_keys, bwd_routes_turns).reshape((SECTIONS, TOKENS, TOPK))
    bwd_weights = jnp.clip(jnp.exp(math.log(1.0) - 1.609438 * jax.random.uniform(splits[5], (SECTIONS, TOKENS, TOPK), jnp.float32) ** levels(splits[5], (SECTIONS, TOKENS, TOPK), ((0, 16), (1, 16)), -0.2, 0.2)), 0.2, 1.0)
    incoming_grad = gaussian(splits[6], (SECTIONS, TOKENS, D), 1.0, 6.0, ((0, 16), (1, 16)))
    norm_gain = jnp.clip(1.0 + 0.18 * jax.random.normal(splits[7], (SECTIONS, D), jnp.float32), 0.1, 1.9)
    gate_proj = gaussian(splits[8], (SECTIONS, EXPERTS, D, FF), D ** -0.5, 0.125, ((0, 16), (1, 16)))
    up_proj = gaussian(splits[9], (SECTIONS, EXPERTS, D, FF), D ** -0.5, 0.125, ((0, 16), (1, 16)))
    down_proj = gaussian(splits[10], (SECTIONS, EXPERTS, FF, D), FF ** -0.5, 0.21875, ((0, 16), (1, 16)))
    return {"fwd_tokens": fwd_tokens, "fwd_routes": fwd_routes, "fwd_weights": fwd_weights, "saved_tokens": saved_tokens, "bwd_routes": bwd_routes, "bwd_weights": bwd_weights, "incoming_grad": incoming_grad, "norm_gain": norm_gain, "gate_proj": gate_proj, "up_proj": up_proj, "down_proj": down_proj}


EPS = 1e-06

def slot_index(route_block, expert_count, capacity):
    flat_route = route_block.reshape(-1)
    chosen = (flat_route[:, None] == jnp.arange(expert_count, dtype=jnp.int32)[None, :]).astype(jnp.int32)
    before = jnp.cumsum(chosen, axis=0) - chosen
    return flat_route * capacity + lax.optimization_barrier(jnp.sum(before * chosen, axis=1))

def buffer_index(route_rows):
    blocks = route_rows.reshape(N_EXPERT, TOK_DEV, TOPK)
    local_slots = jax.vmap(partial(slot_index, expert_count=EXPERTS, capacity=CAP))(blocks)
    flat_route = blocks.reshape(N_EXPERT, TOK_DEV * TOPK)
    slot_number = local_slots - flat_route * CAP
    source_rows = jnp.arange(N_EXPERT, dtype=jnp.int32)[:, None]
    whole_index = flat_route * (N_EXPERT * CAP) + source_rows * CAP + slot_number
    return whole_index.reshape(-1).astype(jnp.int32)

def pack_rows(token_rows, slot_rows):
    spread = jnp.repeat(token_rows, TOPK, axis=0)
    packed = jnp.zeros((EXPERTS * N_EXPERT * CAP, token_rows.shape[1]), token_rows.dtype).at[slot_rows].set(spread)
    return packed.reshape(EXPERTS, N_EXPERT * CAP, token_rows.shape[1])

def unpack_rows(packed, slot_rows):
    flat_rows = packed.reshape((-1,) + packed.shape[2:])
    return flat_rows[slot_rows].reshape((TOKENS, TOPK) + packed.shape[2:])

def matmul(left_rows, right_matrix):
    return jnp.dot(left_rows.astype(jnp.float32), right_matrix.astype(jnp.float32), preferred_element_type=jnp.float32)

def normalize(token_rows, gain_row):
    values = token_rows.astype(jnp.float32)
    inv_scale = lax.rsqrt(lax.optimization_barrier(jnp.mean(values * values, axis=-1, keepdims=True)) + EPS)
    return (values * inv_scale * gain_row, inv_scale)

def expert_forward(operands):
    token_rows, w_gate, w_up, w_down = operands
    gate_pre = matmul(token_rows, w_gate)
    up_pre = matmul(token_rows, w_up)
    hidden = (gate_pre * jax.nn.sigmoid(gate_pre) * up_pre).astype(jnp.bfloat16)
    return matmul(hidden, w_down).astype(jnp.bfloat16)

def expert_backward(operands):
    token_rows, grad_rows, w_gate, w_up, w_down = operands
    gate_pre = matmul(token_rows, w_gate)
    up_pre = matmul(token_rows, w_up)
    sigmoid = jax.nn.sigmoid(gate_pre)
    active = gate_pre * sigmoid
    hidden = (active * up_pre).astype(jnp.bfloat16)
    output = matmul(hidden, w_down).astype(jnp.bfloat16)
    weight_grad = lax.optimization_barrier(jnp.sum(output.astype(jnp.float32) * grad_rows.astype(jnp.float32), axis=1)).astype(jnp.bfloat16)
    hidden_grad = matmul(grad_rows, w_down.T)
    gate_grad = (hidden_grad * up_pre * sigmoid * (1.0 + gate_pre * (1.0 - sigmoid))).astype(jnp.bfloat16)
    up_grad = (hidden_grad * active).astype(jnp.bfloat16)
    row_grad = (matmul(gate_grad, w_gate.T) + matmul(up_grad, w_up.T)).astype(jnp.bfloat16)
    return (row_grad, weight_grad)

def section_pass(operands):
    fwd_rows, fwd_route, fwd_mix, bwd_rows, bwd_route, bwd_mix, grad_rows, gain_row, w_gate, w_up, w_down = operands
    fwd_index = buffer_index(fwd_route)
    normed_fwd, fwd_scale = normalize(fwd_rows, gain_row)
    fwd_packed = pack_rows(normed_fwd.astype(jnp.bfloat16), fwd_index)
    fwd_result = lax.map(expert_forward, (fwd_packed, w_gate, w_up, w_down))
    expert_out = unpack_rows(fwd_result, fwd_index).astype(jnp.float32)
    mixed_rows = fwd_rows.astype(jnp.float32) + lax.optimization_barrier(jnp.sum(fwd_mix[:, :, None] * expert_out, axis=1))
    bwd_index = buffer_index(bwd_route)
    normed_saved, saved_scale = normalize(bwd_rows, gain_row)
    saved_packed = pack_rows(normed_saved.astype(jnp.bfloat16), bwd_index)
    grad_packed = pack_rows(grad_rows, bwd_index)
    row_result, weight_result = lax.map(expert_backward, (saved_packed, grad_packed, w_gate, w_up, w_down))
    choice_grad = unpack_rows(row_result, bwd_index).astype(jnp.float32)
    combine_rows = unpack_rows(weight_result, bwd_index)
    normed_grad = lax.optimization_barrier(jnp.sum(bwd_mix[:, :, None] * choice_grad, axis=1))
    scaled_grad = normed_grad * gain_row
    values = bwd_rows.astype(jnp.float32)
    inner_mean = lax.optimization_barrier(jnp.mean(values * scaled_grad, axis=-1, keepdims=True))
    input_grad = grad_rows.astype(jnp.float32) + saved_scale * scaled_grad - values * saved_scale * saved_scale * saved_scale * inner_mean
    return (mixed_rows.astype(jnp.bfloat16), input_grad.astype(jnp.bfloat16), combine_rows)

def reference(fwd_tokens, fwd_routes, fwd_weights, saved_tokens, bwd_routes, bwd_weights, incoming_grad, norm_gain, gate_proj, up_proj, down_proj):
    mixed, input_grad, combine_grad = lax.map(section_pass, (fwd_tokens, fwd_routes, fwd_weights, saved_tokens, bwd_routes, bwd_weights, incoming_grad, norm_gain, gate_proj, up_proj, down_proj))
    next_input = jnp.roll(mixed, 1, axis=0)
    next_grad = jnp.roll(input_grad, -1, axis=0)
    return (next_input, next_grad, combine_grad)
```

```python
import functools

import jax
import jax.numpy as jnp
from jax import lax
from jax.experimental import pallas as pl
from jax.experimental.pallas import tpu as pltpu
from jax.sharding import PartitionSpec as P

EPS = 1e-06
MESH = pl.DeviceIdType.MESH
F32 = jnp.float32
BF16 = jnp.bfloat16
SLOTS = 32
TOK = 128
RING = 8
REACH = (TOK, TOK, 3 * SLOTS, SLOTS)
SAVED, GRAD, FWD = 0, 1, 2
BWD_ROUTE, FWD_ROUTE = 0, 1
LAST = 7


def block_of(way, hop):
    return LAST if hop == 4 else 3 * way + hop


def iota(shape, dim):
    return lax.broadcasted_iota(jnp.int32, shape, dim)


def dot(a, b):
    return jnp.dot(a, b, preferred_element_type=F32)


def dot_t(a, b):
    return lax.dot_general(a, b, (((1,), (1,)), ((), ())), preferred_element_type=F32)


def hops_of(route, z, x):
    offset = jnp.bitwise_and(route - z + RING, RING - 1)
    other = jnp.where(jnp.right_shift(route, 3) != x, 1, 0)
    half = offset == RING // 2
    plus = jnp.where(offset < RING // 2, offset, jnp.where(half & (other == 0), RING // 2, 0))
    minus = jnp.where(offset > RING // 2, RING - offset, jnp.where(half & (other == 1), RING // 2, 0))
    return (plus, minus), other, offset


def code_of(hop, other):
    return jnp.where(hop > 0, 2 * (hop - 1) + other, -1)


def selector(meta, row):
    slot = iota((SLOTS, TOK), 0).astype(F32) + 1.0
    own = jnp.where(slot == meta[row : row + 1, :], 1.0, 0.0)
    other = jnp.where(slot == meta[row + 1 : row + 2, :], 1.0, 0.0)
    return own, other


def spreader(meta, row):
    own, other = selector(meta, row)
    w_own, w_other = meta[row + 2 : row + 3, :], meta[row + 3 : row + 4, :]
    hi_own, hi_other = w_own.astype(BF16).astype(F32), w_other.astype(BF16).astype(F32)
    stacked = jnp.concatenate(
        [own * hi_own, other * hi_other, own * (w_own - hi_own), other * (w_other - hi_other)], axis=0
    )
    return jnp.transpose(stacked).astype(BF16)


def kernel(
    tokens_f, routes_f, weights_f, tokens_b, routes_b, weights_b, grads, gain, gate_hbm, up_hbm, down_hbm,
    next_input, next_grad, combine,
    packed, r1, r2, r3, r4, meta0, meta1, meta2, meta3, meta4, meta_here, back,
    xsend, xin, w_gate, w_up, w_down, hid_a, hid_b, y_b, y_f, yx_b, yx_f,
    t1, t2, t3, t4, ct_out, ct_in, res, done_f, done_b,
    d_send, d_recv, m_send, m_recv, x_send, x_recv, y_send, y_recv, t_send, t_recv, c_send, c_recv, s_send, s_recv, w_sem,
):
    me = lax.axis_index("expert")
    z, x = lax.rem(me, RING), me // RING
    seg = lax.axis_index("segment")
    sections = lax.axis_size("segment")
    ahead = {"expert": x * RING + lax.rem(z + 1, RING)}
    behind = {"expert": x * RING + lax.rem(z + RING - 1, RING)}
    across = {"expert": (1 - x) * RING + z}
    seg_next = {"segment": lax.rem(seg + 1, sections)}
    seg_prev = {"segment": lax.rem(seg + sections - 1, sections)}
    onward, homeward = (ahead, behind), (behind, ahead)
    width = tokens_f.shape[1]
    hidden = w_gate.shape[1]
    tile = 512
    tiles = width // tile

    loads = [
        pltpu.make_async_copy(src, dst, w_sem.at[i])
        for i, (src, dst) in enumerate(((gate_hbm, w_gate), (up_hbm, w_up), (down_hbm, w_down)))
    ]
    for load in loads:
        load.start()
    barrier = pltpu.get_barrier_semaphore()
    for device in (ahead, behind, across, seg_next, seg_prev):
        pl.semaphore_signal(barrier, inc=1, device_id=device, device_id_type=MESH)

    def over_tiles(body, size=tile):
        @pl.loop(0, width // size)
        def _(i):
            body(pl.ds(pl.multiple_of(i * size, size), size))

    landing = {1: r1, 2: r2, 3: r3}
    returning = {1: t1, 2: t2, 3: t3}
    metas = (meta0, meta1, meta2, meta3, meta4)

    def landed(array, way, hop):
        if hop == 4:
            return r4.at[array, pl.ds(way * SLOTS, SLOTS)]
        return landing[hop].at[array, way]

    def returned(array, way, hop):
        if hop == 4:
            return t4.at[array, pl.ds(way * SLOTS, SLOTS)]
        return returning[hop].at[array, way]

    def remote(src, dst, send, recv, device):
        return pltpu.make_async_remote_copy(
            src_ref=src, dst_ref=dst, send_sem=send, recv_sem=recv, device_id=device, device_id_type=MESH
        )

    def dispatch(array, way, hop):
        source = packed.at[array, way] if hop == 1 else landing[hop - 1].at[array, way]
        rows = REACH[hop - 1]
        at = (array, way, hop - 1)
        return remote(
            source.at[pl.ds(0, rows)], landed(array, way, hop), d_send.at[at], d_recv.at[at], onward[way]
        )

    def meta_copy(route, way, hop):
        at = (route, way, hop - 1)
        return remote(
            metas[hop - 1].at[route, way], metas[hop].at[route, way], m_send.at[at], m_recv.at[at], onward[way]
        )

    def cross(array, block):
        here = pl.ds(block * SLOTS, SLOTS)
        there = pl.ds((8 + block) * SLOTS, SLOTS)
        at = (array, block)
        return remote(xsend.at[array, here], xin.at[array, there], x_send.at[at], x_recv.at[at], across)

    outs, outs_x = (y_b, y_f), (yx_b, yx_f)

    def cross_back(which, block):
        there = pl.ds(block * SLOTS, SLOTS)
        here = pl.ds((8 + block) * SLOTS, SLOTS)
        at = (which, block)
        return remote(
            outs[which].at[here], outs_x[which].at[there], y_send.at[at], y_recv.at[at], across
        )

    reused = (SAVED, FWD)

    def give_back(which, way, hop):
        at = (which, way, hop - 1)
        return remote(
            landed(reused[which], way, hop), returned(which, way, hop), t_send.at[at], t_recv.at[at], homeward[way]
        )

    def give_scalars(way, hop):
        at = (way, hop - 1)
        return remote(ct_out.at[at], ct_in.at[at], c_send.at[at], c_recv.at[at], homeward[way])

    lane = iota((TOK, TOK), 1)
    sub = iota((TOK, TOK), 0)

    def plan(route, routes_ref, weights_ref):
        r_col = [routes_ref[:, k : k + 1] for k in range(2)]
        w_col = [weights_ref[:, k : k + 1] for k in range(2)]
        columns = jnp.zeros((TOK, TOK), F32)
        for j, col in enumerate([r_col[0].astype(F32), r_col[1].astype(F32), w_col[0], w_col[1]]):
            columns = jnp.where(lane == j, col, columns)
        across_rows = jnp.transpose(columns)
        r_row = [across_rows[k : k + 1, :].astype(jnp.int32) for k in range(2)]
        w_row = [across_rows[2 + k : 3 + k, :] for k in range(2)]
        slot_row = []
        for k in range(2):
            earlier = jnp.where((sub < lane) & ((r_col[0] == r_row[k]) | (r_col[1] == r_row[k])), 1.0, 0.0)
            slot_row.append(jnp.sum(earlier, axis=0, keepdims=True) + 1.0)
        info_col = [hops_of(r, z, x) for r in r_col]
        info_row = [hops_of(r, z, x) for r in r_row]
        kind = iota((8, TOK), 0)
        here = jnp.zeros((8, TOK), F32)
        for k in range(2):
            _, other, offset = info_row[k]
            value = jnp.where(kind < 2, slot_row[k], w_row[k])
            here = here + jnp.where((offset == 0) & (jnp.bitwise_and(kind, 1) == other) & (kind < 4), value, 0.0)
        meta_here[route] = here
        j = iota((16, TOK), 0)
        target = 2 * jnp.right_shift(j, 2) + jnp.bitwise_and(j, 1)
        is_slot = jnp.bitwise_and(j, 2) == 0
        orders = []
        for way in range(2):
            far_col = jnp.maximum(info_col[0][0][way], info_col[1][0][way])
            far_row = jnp.maximum(info_row[0][0][way], info_row[1][0][way])
            ahead_of_row = (far_col > far_row) | ((far_col == far_row) & (sub < lane))
            pos_row = jnp.sum(jnp.where(ahead_of_row, 1.0, 0.0), axis=0, keepdims=True)
            ahead_of_col = (far_row > far_col) | ((far_row == far_col) & (lane < sub))
            pos_col = jnp.sum(jnp.where(ahead_of_col, 1.0, 0.0), axis=1, keepdims=True)
            order = jnp.where(sub.astype(F32) == pos_row, 1.0, 0.0).astype(BF16)
            back[route, way] = jnp.where(lane.astype(F32) == pos_col, 1.0, 0.0).astype(BF16)
            meta = jnp.zeros((16, TOK), F32)
            for k in range(2):
                code = code_of(info_row[k][0][way], info_row[k][1])
                meta = meta + jnp.where(code == target, jnp.where(is_slot, slot_row[k], w_row[k]), 0.0)
            high = meta.astype(BF16)
            low = (meta - high.astype(F32)).astype(BF16)
            meta0[route, way] = dot_t(high, order) + dot_t(low, order)
            orders.append(order)
        return orders

    def scale_of(tokens):
        values = tokens[...].astype(F32)
        return lax.rsqrt(jnp.mean(values * values, axis=-1, keepdims=True) + EPS)

    def normalize(tokens, out):
        inv = scale_of(tokens)

        def body(cols):
            out[:, cols] = (tokens[:, cols].astype(F32) * inv * gain[:, cols]).astype(BF16)

        over_tiles(body)

    def pack(array, way, order, rows):
        def body(cols):
            packed[array, way, :, cols] = dot(order, rows[:, cols]).astype(BF16)

        over_tiles(body)

    def pick_here(array, route, rows):
        own, other = selector(meta_here.at[route], 0)
        both = jnp.concatenate([own, other], axis=0).astype(BF16)

        def body(cols):
            picked = dot(both, rows[:, cols]).astype(BF16)
            xin[array, 0:SLOTS, cols] = picked[:SLOTS]
            xsend[array, 0:SLOTS, cols] = picked[SLOTS:]

        over_tiles(body)
        cross(array, 0).start()

    def pick(array, route, ways, hop):
        block = block_of(ways[0], hop)
        rows = REACH[hop - 1]
        at = pl.ds(block * SLOTS, SLOTS)
        matrices = []
        for way in ways:
            own, other = selector(metas[hop].at[route, way], 4 * (hop - 1))
            matrices.append(jnp.concatenate([own, other], axis=0)[:, :rows].astype(BF16))

        def body(cols):
            picked = sum(dot(m, landed(array, w, hop)[:, cols]) for m, w in zip(matrices, ways)).astype(BF16)
            xin[array, at, cols] = picked[:SLOTS]
            xsend[array, at, cols] = picked[SLOTS:]

        over_tiles(body)
        cross(array, block).start()

    def advance(array, hop, route=None):
        for way in range(2):
            if route is not None:
                meta_copy(route, way, hop).wait_recv()
                if hop < 4:
                    meta_copy(route, way, hop + 1).start()
            dispatch(array, way, hop).wait_recv()
            if hop < 4:
                dispatch(array, way, hop + 1).start()

    def pick_all(array, hop, route):
        if hop == 4:
            pick(array, route, (0, 1), 4)
        else:
            pick(array, route, (0,), hop)
            pick(array, route, (1,), hop)

    def spread(which, route, way, hop):
        rows = REACH[hop - 1]
        further = REACH[hop] if hop < 4 else 0
        block = block_of(way, hop)
        at = pl.ds(block * SLOTS, SLOTS)
        meta = metas[hop].at[route, way]
        matrix = spreader(meta, 4 * (hop - 1))[:rows]
        if hop < 4:
            give_back(which, way, hop + 1).wait_recv()
        target = landed(reused[which], way, hop)

        def body(cols):
            own, other = outs[which][at, cols], outs_x[which][at, cols]
            total = dot(matrix, jnp.concatenate([own, other, own, other], axis=0))
            if further:
                came = returned(which, way, hop + 1)[:, cols].astype(F32)
                if further < rows:
                    came = jnp.concatenate([came, jnp.zeros((rows - further, tile), F32)], axis=0)
                total = total + came
            target[:, cols] = total.astype(BF16)

        over_tiles(body)
        give_back(which, way, hop).start()
        if which == 0:
            extra = pl.ds(width, TOK)
            own, other = selector(meta, 4 * (hop - 1))
            scalars = scalar_rows(own, other, y_b[at, extra], yx_b[at, extra], hop)
            if hop < 4:
                give_scalars(way, hop + 1).wait_recv()
                scalars = scalars + ct_in[way, hop]
            ct_out[way, hop - 1] = scalars
            give_scalars(way, hop).start()

    def scalar_rows(own, other, mine, theirs, hop):
        row = iota((8, TOK), 0)
        first = jnp.sum(own * mine.astype(F32), axis=0, keepdims=True)
        second = jnp.sum(other * theirs.astype(F32), axis=0, keepdims=True)
        return jnp.where(row == 2 * (hop - 1), first, jnp.where(row == 2 * (hop - 1) + 1, second, 0.0))

    def gather_sums(which, route):
        matrix = spreader(meta_here.at[route], 0)
        orders = [back[route, way][:, : REACH[0]] for way in range(2)]
        at = pl.ds(0, SLOTS)
        for way in range(2):
            give_back(which, way, 1).wait_recv()

        def body(cols):
            own, other = outs[which][at, cols], outs_x[which][at, cols]
            total = dot(matrix, jnp.concatenate([own, other, own, other], axis=0))
            for way in range(2):
                total = total + dot(orders[way], returned(which, way, 1)[:, cols])
            res[:, cols] = total

        over_tiles(body)

    def backward_hidden():
        @pl.loop(0, hidden // 256)
        def _(i):
            cols = pl.ds(pl.multiple_of(i * 256, 256), 256)
            gate = dot(xin[SAVED], w_gate[:, cols])
            up = dot(xin[SAVED], w_up[:, cols])
            back_in = dot_t(xin[GRAD], w_down[cols, :])
            sigmoid = jax.nn.sigmoid(gate)
            active = gate * sigmoid
            rounded = (active * up).astype(BF16).astype(F32)
            part = jnp.sum(rounded * back_in, axis=1, keepdims=True)
            hid_a[:, cols] = (back_in * up * sigmoid * (1.0 + gate * (1.0 - sigmoid))).astype(BF16)
            hid_b[:, cols] = (back_in * active).astype(BF16)
            res_part = jnp.broadcast_to(part, (part.shape[0], TOK))

            @pl.when(i == 0)
            def _():
                done_b[...] = res_part

            @pl.when(i > 0)
            def _():
                done_b[...] = done_b[...] + res_part

        y_b[:, width : width + TOK] = done_b[...].astype(BF16)

    def backward_rows():
        def body(cols):
            y_b[:, cols] = (dot_t(hid_a[...], w_gate[cols, :]) + dot_t(hid_b[...], w_up[cols, :])).astype(BF16)

        over_tiles(body)

    def forward_hidden():
        @pl.loop(0, hidden // 256)
        def _(i):
            cols = pl.ds(pl.multiple_of(i * 256, 256), 256)
            gate = dot(xin[FWD], w_gate[:, cols])
            up = dot(xin[FWD], w_up[:, cols])
            hid_a[:, cols] = (gate * jax.nn.sigmoid(gate) * up).astype(BF16)

    def forward_rows():
        def body(cols):
            y_f[:, cols] = dot(hid_a[...], w_down[:, cols]).astype(BF16)

        over_tiles(body)

    back_order = (LAST, 3, 6, 2, 5, 1, 4, 0)

    def start_cross_back(which):
        for block in back_order:
            cross_back(which, block).start()

    def wait_cross_back(which, blocks):
        for block in blocks:
            cross_back(which, block).wait_recv()

    orders_b = plan(BWD_ROUTE, routes_b, weights_b)
    normalize(tokens_b, done_f)
    pl.semaphore_wait(barrier, 5)
    for way in range(2):
        meta_copy(BWD_ROUTE, way, 1).start()
    for way in range(2):
        pack(SAVED, way, orders_b[way], done_f)
        dispatch(SAVED, way, 1).start()
    for way in range(2):
        pack(GRAD, way, orders_b[way], grads)
        dispatch(GRAD, way, 1).start()
    pick_here(SAVED, BWD_ROUTE, done_f)
    pick_here(GRAD, BWD_ROUTE, grads)
    orders_f = plan(FWD_ROUTE, routes_f, weights_f)
    normalize(tokens_f, done_f)
    for way in range(2):
        meta_copy(FWD_ROUTE, way, 1).start()
        pack(FWD, way, orders_f[way], done_f)
    pick_here(FWD, FWD_ROUTE, done_f)

    for hop in range(1, 5):
        advance(SAVED, hop, BWD_ROUTE)
        pick_all(SAVED, hop, BWD_ROUTE)
        advance(GRAD, hop)
        if hop == 3:
            for way in range(2):
                dispatch(FWD, way, 1).start()
        pick_all(GRAD, hop, BWD_ROUTE)

    for load in loads:
        load.wait()
    for block in range(8):
        cross(SAVED, block).wait_recv()
        cross(GRAD, block).wait_recv()
    backward_hidden()
    advance(FWD, 1, FWD_ROUTE)
    backward_rows()
    start_cross_back(0)
    for hop in range(1, 5):
        for way in range(2):
            dispatch(SAVED, way, hop).wait_send()
    advance(FWD, 2, FWD_ROUTE)
    wait_cross_back(0, (LAST,))
    for way in range(2):
        spread(0, BWD_ROUTE, way, 4)
    pick_all(FWD, 1, FWD_ROUTE)
    pick_all(FWD, 2, FWD_ROUTE)
    advance(FWD, 3, FWD_ROUTE)
    wait_cross_back(0, (3, 6))
    for way in range(2):
        spread(0, BWD_ROUTE, way, 3)
    pick_all(FWD, 3, FWD_ROUTE)
    advance(FWD, 4, FWD_ROUTE)
    pick_all(FWD, 4, FWD_ROUTE)
    wait_cross_back(0, (2, 5))
    for way in range(2):
        spread(0, BWD_ROUTE, way, 2)
    for block in range(8):
        cross(FWD, block).wait_recv()
    forward_hidden()
    forward_rows()
    start_cross_back(1)
    for hop in range(1, 5):
        for way in range(2):
            dispatch(FWD, way, hop).wait_send()
    wait_cross_back(0, (1, 4, 0))
    wait_cross_back(1, (LAST,))
    for way in range(2):
        spread(1, FWD_ROUTE, way, 4)
    for way in range(2):
        spread(0, BWD_ROUTE, way, 1)
    wait_cross_back(1, (3, 6))
    for way in range(2):
        spread(1, FWD_ROUTE, way, 3)

    def finish_backward():
        gather_sums(0, BWD_ROUTE)
        inv = scale_of(tokens_b)
        scaled = res[...] * gain[...]
        inner = jnp.mean(tokens_b[...].astype(F32) * scaled, axis=-1, keepdims=True)
        cubed = inv * inv * inv * inner

        def body(cols):
            values = tokens_b[:, cols].astype(F32)
            grad = grads[:, cols].astype(F32) + inv * (res[:, cols] * gain[:, cols]) - values * cubed
            packed[0, 0, :, cols] = grad.astype(BF16)

        for way in range(2):
            dispatch(GRAD, way, 1).wait_send()
        over_tiles(body)

    grad_out = remote(packed.at[0, 0], next_grad, s_send.at[0], s_recv.at[0], seg_prev)
    input_out = remote(packed.at[0, 1], next_input, s_send.at[1], s_recv.at[1], seg_next)
    finish_backward()
    grad_out.start()

    wait_cross_back(1, (2, 5))
    for way in range(2):
        spread(1, FWD_ROUTE, way, 2)

    own, other = selector(meta_here.at[BWD_ROUTE], 0)
    at = pl.ds(0, SLOTS)
    extra = pl.ds(width, TOK)
    local = scalar_rows(own, other, y_b[at, extra], yx_b[at, extra], 1)
    unit = jnp.where(lane == sub, 1.0, 0.0).astype(BF16)
    values = [dot_t(unit, local.astype(BF16))]
    for way in range(2):
        give_scalars(way, 1).wait_recv()
        values.append(dot_t(back[BWD_ROUTE, way], ct_in[way, 0].astype(BF16)))
    column = iota((TOK, 8), 1)
    picked = []
    for k in range(2):
        hops, off_column, offset = hops_of(routes_b[:, k : k + 1], z, x)
        codes = [jnp.where(offset == 0, off_column, -1)] + [code_of(hop, off_column) for hop in hops]
        total = sum(jnp.where(code == column, value, 0.0) for code, value in zip(codes, values))
        picked.append(jnp.sum(total, axis=1, keepdims=True))
    combine[...] = jnp.concatenate(picked, axis=1).astype(BF16)

    wait_cross_back(1, (1, 4, 0))
    for way in range(2):
        spread(1, FWD_ROUTE, way, 1)
    gather_sums(1, FWD_ROUTE)

    def body(cols):
        packed[0, 1, :, cols] = (tokens_f[:, cols].astype(F32) + res[:, cols]).astype(BF16)

    over_tiles(body)
    input_out.start()

    for hop in range(1, 5):
        for way in range(2):
            if hop > 1:
                dispatch(GRAD, way, hop).wait_send()
            for route in range(2):
                meta_copy(route, way, hop).wait_send()
                give_back(route, way, hop).wait_send()
            give_scalars(way, hop).wait_send()
    for block in range(8):
        for array in range(3):
            cross(array, block).wait_send()
        for which in range(2):
            cross_back(which, block).wait_send()
    for out in (grad_out, input_out):
        out.wait_send()
        out.wait_recv()


def step(
    fwd_tokens, fwd_routes, fwd_weights, saved_tokens, bwd_routes, bwd_weights, incoming_grad, norm_gain,
    gate_proj, up_proj, down_proj,
):
    rows, width = fwd_tokens.shape[1:]
    hidden = gate_proj.shape[3]
    c1, c2, c3, c4 = REACH
    every = 16 * SLOTS
    vmem = pl.BlockSpec(memory_space=pltpu.VMEM)
    hbm = pl.BlockSpec(memory_space=pl.ANY)
    dma = pltpu.SemaphoreType.DMA
    meta = pltpu.VMEM((2, 2, 16, TOK), F32)
    outs = pl.pallas_call(
        kernel,
        out_shape=(
            jax.ShapeDtypeStruct((rows, width), BF16),
            jax.ShapeDtypeStruct((rows, width), BF16),
            jax.ShapeDtypeStruct((rows, 2), BF16),
        ),
        in_specs=[vmem] * 8 + [hbm] * 3,
        out_specs=(vmem, vmem, vmem),
        scratch_shapes=[
            pltpu.VMEM((3, 2, rows, width), BF16),
            pltpu.VMEM((3, 2, c1, width), BF16),
            pltpu.VMEM((3, 2, c2, width), BF16),
            pltpu.VMEM((3, 2, c3, width), BF16),
            pltpu.VMEM((3, 2 * c4, width), BF16),
            meta, meta, meta, meta, meta,
            pltpu.VMEM((2, 8, TOK), F32),
            pltpu.VMEM((2, 2, TOK, TOK), BF16),
            pltpu.VMEM((3, every // 2, width), BF16),
            pltpu.VMEM((3, every, width), BF16),
            pltpu.VMEM((width, hidden), BF16),
            pltpu.VMEM((width, hidden), BF16),
            pltpu.VMEM((hidden, width), BF16),
            pltpu.VMEM((every, hidden), BF16),
            pltpu.VMEM((every, hidden), BF16),
            pltpu.VMEM((every, width + TOK), BF16),
            pltpu.VMEM((every, width), BF16),
            pltpu.VMEM((every // 2, width + TOK), BF16),
            pltpu.VMEM((every // 2, width), BF16),
            pltpu.VMEM((2, 2, c1, width), BF16),
            pltpu.VMEM((2, 2, c2, width), BF16),
            pltpu.VMEM((2, 2, c3, width), BF16),
            pltpu.VMEM((2, 2 * c4, width), BF16),
            pltpu.VMEM((2, 4, 8, TOK), F32),
            pltpu.VMEM((2, 4, 8, TOK), F32),
            pltpu.VMEM((rows, width), F32),
            pltpu.VMEM((rows, width), BF16),
            pltpu.VMEM((every, TOK), F32),
            dma((3, 2, 4)), dma((3, 2, 4)),
            dma((2, 2, 4)), dma((2, 2, 4)),
            dma((3, 8)), dma((3, 8)),
            dma((2, 8)), dma((2, 8)),
            dma((2, 2, 4)), dma((2, 2, 4)),
            dma((2, 4)), dma((2, 4)),
            dma((2,)), dma((2,)),
            dma((3,)),
        ],
        compiler_params=pltpu.CompilerParams(
            collective_id=0, has_side_effects=True, vmem_limit_bytes=60 * 1024 * 1024
        ),
        cost_estimate=pl.CostEstimate(
            flops=2 * every * width * hidden * 8, bytes_accessed=6 * width * hidden, transcendentals=2 * every * hidden
        ),
    )(
        fwd_tokens[0], fwd_routes[0], fwd_weights[0], saved_tokens[0], bwd_routes[0], bwd_weights[0],
        incoming_grad[0], norm_gain, gate_proj[0, 0], up_proj[0, 0], down_proj[0, 0],
    )
    return tuple(out[None] for out in outs)


def solution(mesh):
    rows = P("segment", "expert", None)
    return jax.shard_map(
        step,
        mesh=mesh,
        in_specs=(rows,) * 7 + (P("segment", None),) + (P("segment", "expert", None, None),) * 3,
        out_specs=(rows, rows, rows),
        check_vma=False,
    )
```

```python
import functools

import jax
import jax.numpy as jnp
from jax import lax
from jax.experimental import pallas as pl
from jax.experimental.pallas import tpu as pltpu
from jax.sharding import PartitionSpec as P

EPS = 1e-06
MESH = pl.DeviceIdType.MESH
F32 = jnp.float32
BF16 = jnp.bfloat16
SLOTS = 32
TOK = 128
RING = 8
TIERS = ((96, 80, 64, SLOTS), (96, 96, 80, SLOTS), (TOK, TOK, 3 * SLOTS, SLOTS))
SAVED, GRAD, FWD = 0, 1, 2
BWD_ROUTE, FWD_ROUTE = 0, 1
PIECES = 4
LAST = 7


def block_of(way, hop):
    return LAST if hop == 4 else 3 * way + hop


def iota(shape, dim):
    return lax.broadcasted_iota(jnp.int32, shape, dim)


def dot(a, b):
    return jnp.dot(a, b, preferred_element_type=F32)


def dot_t(a, b):
    return lax.dot_general(a, b, (((1,), (1,)), ((), ())), preferred_element_type=F32)


def place_of(route, z, x):
    offset = jnp.bitwise_and(route - z + RING, RING - 1)
    return offset, jnp.where(jnp.right_shift(route, 3) != x, 1, 0)


def hops_of(route, forth, z, x):
    offset, other = place_of(route, z, x)
    half = offset == RING // 2
    forth = other == 0 if forth is None else forth == 1
    plus = jnp.where(offset < RING // 2, offset, jnp.where(half & forth, RING // 2, 0))
    minus = jnp.where(offset > RING // 2, RING - offset, jnp.where(half & jnp.logical_not(forth), RING // 2, 0))
    return (plus, minus), other, offset


def agree(
    routes_b, routes_f, plan, tier, first, second, send, recv
):
    me, seg = lax.axis_index("expert"), lax.axis_index("segment")
    experts, sections = lax.axis_size("expert"), lax.axis_size("segment")
    z, x = lax.rem(me, RING), me // RING
    barrier = pltpu.get_barrier_semaphore()
    for step in range(1, experts):
        peer = {"expert": lax.rem(me + step, experts)}
        pl.semaphore_signal(barrier, inc=1, device_id=peer, device_id_type=MESH)
    for step in range(1, sections):
        peer = {"segment": lax.rem(seg + step, sections)}
        pl.semaphore_signal(barrier, inc=1, device_id=peer, device_id_type=MESH)

    row = iota((8, 1), 0)
    cap = [jnp.zeros((8, 1), F32), jnp.zeros((8, 1), F32)]
    for hop in range(4):
        for i in range(2):
            cap[i] = jnp.where(jnp.bitwise_and(row, 3) == hop, float(TIERS[i][hop]), cap[i])
    need = jnp.zeros((1, 1), F32)
    ways = []
    for routes in (routes_b, routes_f):
        places = [place_of(routes[k : k + 1, :], z, x) for k in range(2)]
        base = [jnp.zeros((1, TOK), jnp.int32)] * 2
        for offset, _ in places:
            base[0] = jnp.maximum(base[0], jnp.where(offset < 4, offset, 0))
            base[1] = jnp.maximum(base[1], jnp.where(offset > 4, RING - offset, 0))
        best = None
        for option in range(4):
            forths, far = [], list(base)
            for k in range(2):
                offset, other = places[k]
                beside = places[1 - k][0]
                free = jnp.where(other == 0, option % 2, option // 2)
                forth = jnp.where((beside > 0) & (beside < 4), 1, jnp.where(beside > 4, 0, free))
                far[0] = jnp.where((offset == 4) & (forth == 1), 4, far[0])
                far[1] = jnp.where((offset == 4) & (forth == 0), 4, far[1])
                forths.append(forth)
            reach = jnp.where(iota((8, TOK), 0) < 4, far[0], far[1])
            goes = jnp.where(reach > jnp.bitwise_and(iota((8, TOK), 0), 3), 1.0, 0.0)
            count = jnp.sum(goes, axis=1, keepdims=True)
            over = [jnp.sum(jnp.maximum(count - c, 0.0), axis=0, keepdims=True) for c in cap]
            score = over[1] * 65536.0 + over[0] * 1024.0 + jnp.sum(count, axis=0, keepdims=True)
            if best is None:
                best = (score, over, forths)
            else:
                take = score < best[0]
                best = (
                    jnp.where(take, score, best[0]),
                    [jnp.where(take, new, old) for new, old in zip(over, best[1])],
                    [jnp.where(take, new, old) for new, old in zip(forths, best[2])],
                )
        own = jnp.where(best[1][1] > 0, 2.0, jnp.where(best[1][0] > 0, 1.0, 0.0))
        need = jnp.maximum(need, own)
        ways += best[2]
    rows = iota((8, TOK), 0)
    table = jnp.zeros((8, TOK), jnp.int32)
    for i, way in enumerate(ways):
        table = jnp.where(rows == i, way, table)
    plan[...] = table

    pl.semaphore_wait(barrier, experts + sections - 2)
    first[0] = jnp.broadcast_to(need, (8, TOK))
    for axis, index, size, held, at in (("expert", me, experts, first, 0), ("segment", seg, sections, second, 1)):
        copies = [
            pltpu.make_async_remote_copy(
                src_ref=held.at[0], dst_ref=held.at[step], send_sem=send.at[at, step], recv_sem=recv.at[at, step],
                device_id={axis: lax.rem(index + step, size)}, device_id_type=MESH,
            )
            for step in range(1, size)
        ]
        for copy in copies:
            copy.start()
        total = held[0]
        for step, copy in enumerate(copies):
            copy.wait_recv()
            total = jnp.maximum(total, held[step + 1])
        if at == 0:
            second[0] = total
        else:
            tier[...] = total.astype(jnp.int32)
        for copy in copies:
            copy.wait_send()


def code_of(hop, other):
    return jnp.where(hop > 0, 2 * (hop - 1) + other, -1)


def selector(meta, row):
    slot = iota((SLOTS, TOK), 0).astype(F32) + 1.0
    own = jnp.where(slot == meta[row : row + 1, :], 1.0, 0.0)
    other = jnp.where(slot == meta[row + 1 : row + 2, :], 1.0, 0.0)
    return own, other


def spreader(meta, row):
    own, other = selector(meta, row)
    w_own, w_other = meta[row + 2 : row + 3, :], meta[row + 3 : row + 4, :]
    hi_own, hi_other = w_own.astype(BF16).astype(F32), w_other.astype(BF16).astype(F32)
    stacked = jnp.concatenate(
        [own * hi_own, other * hi_other, own * (w_own - hi_own), other * (w_other - hi_other)], axis=0
    )
    return jnp.transpose(stacked).astype(BF16)


def kernel(
    reach, general, plan_ref, tokens_f, routes_f, weights_f, tokens_b, routes_b, weights_b, grads, gain, gate_hbm, up_hbm, down_hbm,
    next_input, next_grad, combine,
    packed, r1, r2, r3, r4, meta0, meta1, meta2, meta3, meta4, meta_here, back,
    xsend, xin, w_gate, w_up, w_down, hid_a, hid_b, y_b, y_f, yx_b, yx_f,
    t1, t2, t3, t4, ct_out, ct_in, res, done_f, done_b,
    d_send, d_recv, m_send, m_recv, x_send, x_recv, y_send, y_recv, t_send, t_recv, c_send, c_recv, s_send, s_recv, w_sem,
):
    me = lax.axis_index("expert")
    z, x = lax.rem(me, RING), me // RING
    seg = lax.axis_index("segment")
    sections = lax.axis_size("segment")
    ahead = {"expert": x * RING + lax.rem(z + 1, RING)}
    behind = {"expert": x * RING + lax.rem(z + RING - 1, RING)}
    across = {"expert": (1 - x) * RING + z}
    seg_next = {"segment": lax.rem(seg + 1, sections)}
    seg_prev = {"segment": lax.rem(seg + sections - 1, sections)}
    onward, homeward = (ahead, behind), (behind, ahead)
    width = tokens_f.shape[1]
    hidden = w_gate.shape[1]
    tile = 512
    tiles = width // tile

    loads = [
        pltpu.make_async_copy(src, dst, w_sem.at[i])
        for i, (src, dst) in enumerate(((gate_hbm, w_gate), (up_hbm, w_up), (down_hbm, w_down)))
    ]
    for load in loads:
        load.start()
    barrier = pltpu.get_barrier_semaphore()
    for device in (ahead, behind, across, seg_next, seg_prev):
        pl.semaphore_signal(barrier, inc=1, device_id=device, device_id_type=MESH)

    def over_tiles(body, size=tile):
        @pl.loop(0, width // size)
        def _(i):
            body(pl.ds(pl.multiple_of(i * size, size), size))

    landing = {1: r1, 2: r2, 3: r3}
    returning = {1: t1, 2: t2, 3: t3}
    metas = (meta0, meta1, meta2, meta3, meta4)

    def landed(array, way, hop):
        if hop == 4:
            return r4.at[array, pl.ds(way * SLOTS, SLOTS)]
        return landing[hop].at[array, way]

    def returned(array, way, hop):
        if hop == 4:
            return t4.at[array, pl.ds(way * SLOTS, SLOTS)]
        return returning[hop].at[array, way]

    def remote(src, dst, send, recv, device):
        return pltpu.make_async_remote_copy(
            src_ref=src, dst_ref=dst, send_sem=send, recv_sem=recv, device_id=device, device_id_type=MESH
        )

    def dispatch(array, way, hop):
        source = packed.at[array, way] if hop == 1 else landing[hop - 1].at[array, way]
        rows = reach[hop - 1]
        at = (array, way, hop - 1)
        return remote(
            source.at[pl.ds(0, rows)], landed(array, way, hop), d_send.at[at], d_recv.at[at], onward[way]
        )

    def meta_copy(route, way, hop):
        at = (route, way, hop - 1)
        return remote(
            metas[hop - 1].at[route, way], metas[hop].at[route, way], m_send.at[at], m_recv.at[at], onward[way]
        )

    def cross(array, block):
        here = pl.ds(block * SLOTS, SLOTS)
        there = pl.ds((8 + block) * SLOTS, SLOTS)
        at = (array, block)
        return remote(xsend.at[array, here], xin.at[array, there], x_send.at[at], x_recv.at[at], across)

    outs, outs_x = (y_b, y_f), (yx_b, yx_f)

    def cross_back(which, block):
        there = pl.ds(block * SLOTS, SLOTS)
        here = pl.ds((8 + block) * SLOTS, SLOTS)
        at = (which, block)
        return remote(
            outs[which].at[here], outs_x[which].at[there], y_send.at[at], y_recv.at[at], across
        )

    reused = (SAVED, FWD)

    def piece_of(piece):
        return pl.ds(piece * (width // PIECES), width // PIECES)

    def give_back(which, way, hop, piece):
        at = (which, way, hop - 1, piece)
        cols = piece_of(piece)
        return remote(
            landed(reused[which], way, hop).at[:, cols], returned(which, way, hop).at[:, cols],
            t_send.at[at], t_recv.at[at], homeward[way],
        )

    def give_scalars(way, hop):
        at = (way, hop - 1)
        return remote(ct_out.at[at], ct_in.at[at], c_send.at[at], c_recv.at[at], homeward[way])

    lane = iota((TOK, TOK), 1)
    sub = iota((TOK, TOK), 0)

    def columns_of(rows):
        stacked = jnp.zeros((TOK, TOK), F32)
        for k, row in enumerate(rows):
            stacked = jnp.where(sub == k, row.astype(F32), stacked)
        turned = jnp.transpose(stacked)
        return [turned[:, k : k + 1].astype(jnp.int32) for k in range(len(rows))]

    def forths_of(route):
        return [None if general else plan_ref[2 * route + k : 2 * route + k + 1, :] for k in range(2)]

    def route_columns(r_row, f_row):
        if general:
            return columns_of(r_row), f_row
        columns = columns_of(r_row + f_row)
        return columns[:2], columns[2:]

    def plan(route, routes_ref, weights_ref):
        r_row = [routes_ref[k : k + 1, :] for k in range(2)]
        w_row = [weights_ref[k : k + 1, :] for k in range(2)]
        f_row = forths_of(route)
        r_col, f_col = route_columns(r_row, f_row)
        slot_row = []
        for k in range(2):
            earlier = jnp.where((sub < lane) & ((r_col[0] == r_row[k]) | (r_col[1] == r_row[k])), 1.0, 0.0)
            slot_row.append(jnp.sum(earlier, axis=0, keepdims=True) + 1.0)
        info_col = [hops_of(r, f, z, x) for r, f in zip(r_col, f_col)]
        info_row = [hops_of(r, f, z, x) for r, f in zip(r_row, f_row)]
        kind = iota((8, TOK), 0)
        here = jnp.zeros((8, TOK), F32)
        for k in range(2):
            _, other, offset = info_row[k]
            value = jnp.where(kind < 2, slot_row[k], w_row[k])
            here = here + jnp.where((offset == 0) & (jnp.bitwise_and(kind, 1) == other) & (kind < 4), value, 0.0)
        meta_here[route] = here
        j = iota((16, TOK), 0)
        target = 2 * jnp.right_shift(j, 2) + jnp.bitwise_and(j, 1)
        is_slot = jnp.bitwise_and(j, 2) == 0
        orders = []
        for way in range(2):
            far_col = jnp.maximum(info_col[0][0][way], info_col[1][0][way])
            far_row = jnp.maximum(info_row[0][0][way], info_row[1][0][way])
            ahead_of_row = (far_col > far_row) | ((far_col == far_row) & (sub < lane))
            pos_row = jnp.sum(jnp.where(ahead_of_row, 1.0, 0.0), axis=0, keepdims=True)
            ahead_of_col = (far_row > far_col) | ((far_row == far_col) & (lane < sub))
            pos_col = jnp.sum(jnp.where(ahead_of_col, 1.0, 0.0), axis=1, keepdims=True)
            order = jnp.where(sub.astype(F32) == pos_row, 1.0, 0.0).astype(BF16)
            back[route, way] = jnp.where(lane.astype(F32) == pos_col, 1.0, 0.0).astype(BF16)
            meta = jnp.zeros((16, TOK), F32)
            for k in range(2):
                code = code_of(info_row[k][0][way], info_row[k][1])
                meta = meta + jnp.where(code == target, jnp.where(is_slot, slot_row[k], w_row[k]), 0.0)
            high = meta.astype(BF16)
            low = (meta - high.astype(F32)).astype(BF16)
            meta0[route, way] = dot_t(high, order) + dot_t(low, order)
            orders.append(order)
        return orders

    def scale_of(tokens):
        values = tokens[...].astype(F32)
        return lax.rsqrt(jnp.mean(values * values, axis=-1, keepdims=True) + EPS)

    def normalize(tokens, out):
        inv = scale_of(tokens)

        def body(cols):
            out[:, cols] = (tokens[:, cols].astype(F32) * inv * gain[:, cols]).astype(BF16)

        over_tiles(body)

    def pack(array, way, order, rows):
        def body(cols):
            packed[array, way, 0 : reach[0], cols] = dot(order[: reach[0]], rows[:, cols]).astype(BF16)

        over_tiles(body)

    def pick_here(array, route, rows):
        own, other = selector(meta_here.at[route], 0)
        both = jnp.concatenate([own, other], axis=0).astype(BF16)

        def body(cols):
            picked = dot(both, rows[:, cols]).astype(BF16)
            xin[array, 0:SLOTS, cols] = picked[:SLOTS]
            xsend[array, 0:SLOTS, cols] = picked[SLOTS:]

        over_tiles(body)
        cross(array, 0).start()

    def pick(array, route, ways, hop):
        block = block_of(ways[0], hop)
        rows = reach[hop - 1]
        at = pl.ds(block * SLOTS, SLOTS)
        matrices = []
        for way in ways:
            own, other = selector(metas[hop].at[route, way], 4 * (hop - 1))
            matrices.append(jnp.concatenate([own, other], axis=0)[:, :rows].astype(BF16))

        def body(cols):
            picked = sum(dot(m, landed(array, w, hop)[:, cols]) for m, w in zip(matrices, ways)).astype(BF16)
            xin[array, at, cols] = picked[:SLOTS]
            xsend[array, at, cols] = picked[SLOTS:]

        over_tiles(body)
        cross(array, block).start()

    def advance(array, hop, route=None):
        for way in range(2):
            if route is not None:
                meta_copy(route, way, hop).wait_recv()
                if hop < 4:
                    meta_copy(route, way, hop + 1).start()
            dispatch(array, way, hop).wait_recv()
            if hop < 4:
                dispatch(array, way, hop + 1).start()

    def pick_all(array, hop, route):
        if hop == 4:
            pick(array, route, (0, 1), 4)
        else:
            pick(array, route, (0,), hop)
            pick(array, route, (1,), hop)

    def spread(which, route, hop):
        rows = reach[hop - 1]
        further = reach[hop] if hop < 4 else 0
        blocks = [pl.ds(block_of(way, hop) * SLOTS, SLOTS) for way in range(2)]
        matrices = [spreader(metas[hop].at[route, way], 4 * (hop - 1))[:rows] for way in range(2)]
        for piece in range(PIECES):
            cols = piece_of(piece)
            for way, at, matrix in zip(range(2), blocks, matrices):
                own, other = outs[which][at, cols], outs_x[which][at, cols]
                total = dot(matrix, jnp.concatenate([own, other, own, other], axis=0))
                if further:
                    give_back(which, way, hop + 1, piece).wait_recv()
                    came = returned(which, way, hop + 1)[:, cols].astype(F32)
                    if further < rows:
                        came = jnp.concatenate([came, jnp.zeros((rows - further, width // PIECES), F32)], axis=0)
                    total = total + came
                landed(reused[which], way, hop)[:, cols] = total.astype(BF16)
                give_back(which, way, hop, piece).start()
        if which == 0:
            extra = pl.ds(width, TOK)
            for way, at in zip(range(2), blocks):
                own, other = selector(metas[hop].at[route, way], 4 * (hop - 1))
                scalars = scalar_rows(own, other, y_b[at, extra], yx_b[at, extra], hop)
                if hop < 4:
                    give_scalars(way, hop + 1).wait_recv()
                    scalars = scalars + ct_in[way, hop]
                ct_out[way, hop - 1] = scalars
                give_scalars(way, hop).start()

    def scalar_rows(own, other, mine, theirs, hop):
        row = iota((8, TOK), 0)
        first = jnp.sum(own * mine.astype(F32), axis=0, keepdims=True)
        second = jnp.sum(other * theirs.astype(F32), axis=0, keepdims=True)
        return jnp.where(row == 2 * (hop - 1), first, jnp.where(row == 2 * (hop - 1) + 1, second, 0.0))

    def gather_sums(which, route, use):
        matrix = spreader(meta_here.at[route], 0)
        orders = [back[route, way][:, : reach[0]] for way in range(2)]
        at = pl.ds(0, SLOTS)
        for piece in range(PIECES):
            cols = piece_of(piece)
            own, other = outs[which][at, cols], outs_x[which][at, cols]
            total = dot(matrix, jnp.concatenate([own, other, own, other], axis=0))
            for way in range(2):
                give_back(which, way, 1, piece).wait_recv()
                total = total + dot(orders[way], returned(which, way, 1)[:, cols])
            use(piece, cols, total)

    def backward_hidden(first, last):
        @pl.loop(first, last)
        def _(i):
            cols = pl.ds(pl.multiple_of(i * 256, 256), 256)
            gate = dot(xin[SAVED], w_gate[:, cols])
            up = dot(xin[SAVED], w_up[:, cols])
            back_in = dot_t(xin[GRAD], w_down[cols, :])
            sigmoid = jax.nn.sigmoid(gate)
            active = gate * sigmoid
            rounded = (active * up).astype(BF16).astype(F32)
            part = jnp.sum(rounded * back_in, axis=1, keepdims=True)
            hid_a[:, cols] = (back_in * up * sigmoid * (1.0 + gate * (1.0 - sigmoid))).astype(BF16)
            hid_b[:, cols] = (back_in * active).astype(BF16)
            res_part = jnp.broadcast_to(part, (part.shape[0], TOK))

            @pl.when(i == 0)
            def _():
                done_b[...] = res_part

            @pl.when(i > 0)
            def _():
                done_b[...] = done_b[...] + res_part

    def backward_rows():
        y_b[:, width : width + TOK] = done_b[...].astype(BF16)

        def body(cols):
            y_b[:, cols] = (dot_t(hid_a[...], w_gate[cols, :]) + dot_t(hid_b[...], w_up[cols, :])).astype(BF16)

        over_tiles(body)

    def forward_hidden():
        @pl.loop(0, hidden // 256)
        def _(i):
            cols = pl.ds(pl.multiple_of(i * 256, 256), 256)
            gate = dot(xin[FWD], w_gate[:, cols])
            up = dot(xin[FWD], w_up[:, cols])
            hid_a[:, cols] = (gate * jax.nn.sigmoid(gate) * up).astype(BF16)

    def forward_rows():
        def body(cols):
            y_f[:, cols] = dot(hid_a[...], w_down[:, cols]).astype(BF16)

        over_tiles(body)

    back_order = (LAST, 3, 6, 2, 5, 1, 4, 0)

    def start_cross_back(which):
        for block in back_order:
            cross_back(which, block).start()

    def wait_cross_back(which, blocks):
        for block in blocks:
            cross_back(which, block).wait_recv()

    orders_b = plan(BWD_ROUTE, routes_b, weights_b)
    for way in range(2):
        pack(GRAD, way, orders_b[way], grads)
    pl.semaphore_wait(barrier, 5)
    for way in range(2):
        dispatch(GRAD, way, 1).start()
    for way in range(2):
        meta_copy(BWD_ROUTE, way, 1).start()
    normalize(tokens_b, done_f)
    for way in range(2):
        pack(SAVED, way, orders_b[way], done_f)
        dispatch(SAVED, way, 1).start()
    pick_here(GRAD, BWD_ROUTE, grads)
    pick_here(SAVED, BWD_ROUTE, done_f)

    def prepare_forward():
        orders_f = plan(FWD_ROUTE, routes_f, weights_f)
        normalize(tokens_f, done_f)
        for way in range(2):
            meta_copy(FWD_ROUTE, way, 1).start()
            pack(FWD, way, orders_f[way], done_f)
        pick_here(FWD, FWD_ROUTE, done_f)

    for hop in range(1, 5):
        advance(GRAD, hop, BWD_ROUTE)
        pick_all(GRAD, hop, BWD_ROUTE)
        advance(SAVED, hop)
        if hop == 3:
            for way in range(2):
                dispatch(FWD, way, 1).start()
        pick_all(SAVED, hop, BWD_ROUTE)
        if hop == 1:
            prepare_forward()

    for load in loads:
        load.wait()
    for block in range(8):
        cross(SAVED, block).wait_recv()
        cross(GRAD, block).wait_recv()
    steps = hidden // 256
    backward_hidden(0, steps - 1)
    advance(FWD, 1, FWD_ROUTE)
    backward_hidden(steps - 1, steps)
    backward_rows()
    start_cross_back(0)
    for hop in range(1, 5):
        for way in range(2):
            dispatch(SAVED, way, hop).wait_send()
    advance(FWD, 2, FWD_ROUTE)
    wait_cross_back(0, (LAST,))
    spread(0, BWD_ROUTE, 4)
    pick_all(FWD, 1, FWD_ROUTE)
    pick_all(FWD, 2, FWD_ROUTE)
    advance(FWD, 3, FWD_ROUTE)
    wait_cross_back(0, (3, 6))
    spread(0, BWD_ROUTE, 3)
    pick_all(FWD, 3, FWD_ROUTE)
    advance(FWD, 4, FWD_ROUTE)
    pick_all(FWD, 4, FWD_ROUTE)
    wait_cross_back(0, (2, 5))
    spread(0, BWD_ROUTE, 2)
    for block in range(8):
        cross(FWD, block).wait_recv()
    forward_hidden()
    forward_rows()
    start_cross_back(1)
    for hop in range(1, 5):
        for way in range(2):
            dispatch(FWD, way, hop).wait_send()
    wait_cross_back(1, (LAST,))
    spread(1, FWD_ROUTE, 4)
    wait_cross_back(0, (1, 4, 0))
    spread(0, BWD_ROUTE, 1)
    wait_cross_back(1, (3, 6))
    spread(1, FWD_ROUTE, 3)

    def finish_backward():
        def keep(piece, cols, total):
            res[:, cols] = total

        gather_sums(0, BWD_ROUTE, keep)
        inv = scale_of(tokens_b)
        scaled = res[...] * gain[...]
        inner = jnp.mean(tokens_b[...].astype(F32) * scaled, axis=-1, keepdims=True)
        cubed = inv * inv * inv * inner

        def body(cols):
            values = tokens_b[:, cols].astype(F32)
            grad = grads[:, cols].astype(F32) + inv * (res[:, cols] * gain[:, cols]) - values * cubed
            packed[0, 0, :, cols] = grad.astype(BF16)

        for way in range(2):
            dispatch(GRAD, way, 1).wait_send()
        over_tiles(body)

    grad_out = remote(packed.at[0, 0], next_grad, s_send.at[0], s_recv.at[0], seg_prev)

    def input_out(piece):
        cols = piece_of(piece)
        at = 1 + piece
        return remote(packed.at[0, 1, :, cols], next_input.at[:, cols], s_send.at[at], s_recv.at[at], seg_next)

    finish_backward()
    grad_out.start()

    wait_cross_back(1, (2, 5))
    spread(1, FWD_ROUTE, 2)

    own, other = selector(meta_here.at[BWD_ROUTE], 0)
    at = pl.ds(0, SLOTS)
    extra = pl.ds(width, TOK)
    local = scalar_rows(own, other, y_b[at, extra], yx_b[at, extra], 1)
    unit = jnp.where(lane == sub, 1.0, 0.0).astype(BF16)
    values = [dot_t(unit, local.astype(BF16))]
    for way in range(2):
        give_scalars(way, 1).wait_recv()
        values.append(dot_t(back[BWD_ROUTE, way], ct_in[way, 0].astype(BF16)))
    column = iota((TOK, 8), 1)
    picked = jnp.zeros((TOK, TOK), F32)
    columns = route_columns([routes_b[k : k + 1, :] for k in range(2)], forths_of(BWD_ROUTE))
    for k in range(2):
        hops, off_column, offset = hops_of(columns[0][k], columns[1][k], z, x)
        codes = [jnp.where(offset == 0, off_column, -1)] + [code_of(hop, off_column) for hop in hops]
        total = sum(jnp.where(code == column, value, 0.0) for code, value in zip(codes, values))
        picked = jnp.where(lane == k, jnp.sum(total, axis=1, keepdims=True), picked)
    combine[...] = jnp.transpose(picked)[:2, :].astype(BF16)

    wait_cross_back(1, (1, 4, 0))
    spread(1, FWD_ROUTE, 1)

    def finish_forward(piece, cols, total):
        packed[0, 1, :, cols] = (tokens_f[:, cols].astype(F32) + total).astype(BF16)
        input_out(piece).start()

    gather_sums(1, FWD_ROUTE, finish_forward)

    for hop in range(1, 5):
        for way in range(2):
            if hop > 1:
                dispatch(GRAD, way, hop).wait_send()
            for route in range(2):
                meta_copy(route, way, hop).wait_send()
                for piece in range(PIECES):
                    give_back(route, way, hop, piece).wait_send()
            give_scalars(way, hop).wait_send()
    for block in range(8):
        for array in range(3):
            cross(array, block).wait_send()
        for which in range(2):
            cross_back(which, block).wait_send()
    for out in [grad_out] + [input_out(piece) for piece in range(PIECES)]:
        out.wait_send()
        out.wait_recv()


def hand_over(*refs):
    half = len(refs) // 2
    for source, target in zip(refs[:half], refs[half:]):
        target[...] = source[...]


def pass_through(number, rows, width, hidden):
    c1, c2, c3, c4 = TIERS[number]
    every = 16 * SLOTS
    vmem = pl.BlockSpec(memory_space=pltpu.VMEM)
    hbm = pl.BlockSpec(memory_space=pl.ANY)
    dma = pltpu.SemaphoreType.DMA
    meta = pltpu.VMEM((2, 2, 16, TOK), F32)
    return pl.pallas_call(
        functools.partial(kernel, TIERS[number], number == len(TIERS) - 1),
        out_shape=(
            jax.ShapeDtypeStruct((rows, width), BF16),
            jax.ShapeDtypeStruct((rows, width), BF16),
            jax.ShapeDtypeStruct((2, rows), BF16),
        ),
        in_specs=[vmem] * 9 + [hbm] * 3,
        out_specs=(vmem, vmem, vmem),
        scratch_shapes=[
            pltpu.VMEM((3, 2, rows, width), BF16),
            pltpu.VMEM((3, 2, c1, width), BF16),
            pltpu.VMEM((3, 2, c2, width), BF16),
            pltpu.VMEM((3, 2, c3, width), BF16),
            pltpu.VMEM((3, 2 * c4, width), BF16),
            meta, meta, meta, meta, meta,
            pltpu.VMEM((2, 8, TOK), F32),
            pltpu.VMEM((2, 2, TOK, TOK), BF16),
            pltpu.VMEM((3, every // 2, width), BF16),
            pltpu.VMEM((3, every, width), BF16),
            pltpu.VMEM((width, hidden), BF16),
            pltpu.VMEM((width, hidden), BF16),
            pltpu.VMEM((hidden, width), BF16),
            pltpu.VMEM((every, hidden), BF16),
            pltpu.VMEM((every, hidden), BF16),
            pltpu.VMEM((every, width + TOK), BF16),
            pltpu.VMEM((every, width), BF16),
            pltpu.VMEM((every // 2, width + TOK), BF16),
            pltpu.VMEM((every // 2, width), BF16),
            pltpu.VMEM((2, 2, c1, width), BF16),
            pltpu.VMEM((2, 2, c2, width), BF16),
            pltpu.VMEM((2, 2, c3, width), BF16),
            pltpu.VMEM((2, 2 * c4, width), BF16),
            pltpu.VMEM((2, 4, 8, TOK), F32),
            pltpu.VMEM((2, 4, 8, TOK), F32),
            pltpu.VMEM((rows, width), F32),
            pltpu.VMEM((rows, width), BF16),
            pltpu.VMEM((every, TOK), F32),
            dma((3, 2, 4)), dma((3, 2, 4)),
            dma((2, 2, 4)), dma((2, 2, 4)),
            dma((3, 8)), dma((3, 8)),
            dma((2, 8)), dma((2, 8)),
            dma((2, 2, 4, PIECES)), dma((2, 2, 4, PIECES)),
            dma((2, 4)), dma((2, 4)),
            dma((1 + PIECES,)), dma((1 + PIECES,)),
            dma((3,)),
        ],
        compiler_params=pltpu.CompilerParams(
            collective_id=1 + number, has_side_effects=True, vmem_limit_bytes=60 * 1024 * 1024
        ),
        cost_estimate=pl.CostEstimate(
            flops=2 * every * width * hidden * 8, bytes_accessed=6 * width * hidden, transcendentals=2 * every * hidden
        ),
    )


def step(
    fwd_tokens, fwd_routes, fwd_weights, saved_tokens, bwd_routes, bwd_weights, incoming_grad, norm_gain,
    gate_proj, up_proj, down_proj,
):
    rows, width = fwd_tokens.shape[1:]
    hidden = gate_proj.shape[3]
    vmem = pl.BlockSpec(memory_space=pltpu.VMEM)
    dma = pltpu.SemaphoreType.DMA
    experts, sections = lax.axis_size("expert"), lax.axis_size("segment")
    most = max(experts, sections)
    routes_f, routes_b = fwd_routes[0].T, bwd_routes[0].T
    table = jax.ShapeDtypeStruct((8, TOK), jnp.int32)
    plan, tier = pl.pallas_call(
        agree,
        out_shape=(table, table),
        in_specs=[vmem, vmem],
        out_specs=(vmem, vmem),
        scratch_shapes=[
            pltpu.VMEM((experts, 8, TOK), F32),
            pltpu.VMEM((sections, 8, TOK), F32),
            dma((2, most)), dma((2, most)),
        ],
        compiler_params=pltpu.CompilerParams(collective_id=0, has_side_effects=True),
    )(routes_b, routes_f)
    outs = lax.switch(
        tier[0, 0],
        [pass_through(number, rows, width, hidden) for number in range(len(TIERS))],
        plan, fwd_tokens[0], routes_f, fwd_weights[0].T, saved_tokens[0], routes_b, bwd_weights[0].T,
        incoming_grad[0], norm_gain, gate_proj[0, 0], up_proj[0, 0], down_proj[0, 0],
    )
    outs = pl.pallas_call(
        hand_over,
        out_shape=tuple(jax.ShapeDtypeStruct(out.shape, out.dtype) for out in outs),
        in_specs=[vmem] * 3,
        out_specs=(vmem,) * 3,
    )(*outs)
    return (outs[0][None], outs[1][None], outs[2].T[None])


def solution(mesh):
    rows = P("segment", "expert", None)
    return jax.shard_map(
        step,
        mesh=mesh,
        in_specs=(rows,) * 7 + (P("segment", None),) + (P("segment", "expert", None, None),) * 3,
        out_specs=(rows, rows, rows),
        check_vma=False,
    )
```

```python
import functools

import jax
import jax.numpy as jnp
from jax import lax
from jax.experimental import pallas as pl
from jax.experimental.pallas import tpu as pltpu
from jax.sharding import PartitionSpec as P

EPS = 1e-06
MESH = pl.DeviceIdType.MESH
F32 = jnp.float32
BF16 = jnp.bfloat16
SLOTS = 32
TOK = 128
RING = 8
TIERS = ((96, 96, 80, SLOTS), (TOK, TOK, 3 * SLOTS, SLOTS))
SAVED, GRAD, FWD = 0, 1, 2
BWD_ROUTE, FWD_ROUTE = 0, 1
PIECES = 4
GROUPS = (("expert", 1, 16), ("segment", 1, 16))
LAST = 7


def block_of(way, hop):
    return LAST if hop == 4 else 3 * way + hop


def iota(shape, dim):
    return lax.broadcasted_iota(jnp.int32, shape, dim)


def dot(a, b):
    return jnp.dot(a, b, preferred_element_type=F32)


def dot_t(a, b):
    return lax.dot_general(a, b, (((1,), (1,)), ((), ())), preferred_element_type=F32)


def place_of(route, z, x):
    offset = jnp.bitwise_and(route - z + RING, RING - 1)
    return offset, jnp.where(jnp.right_shift(route, 3) != x, 1, 0)


def hops_of(route, forth, z, x):
    offset, other = place_of(route, z, x)
    half = offset == RING // 2
    forth = other == 0 if forth is None else forth == 1
    plus = jnp.where(offset < RING // 2, offset, jnp.where(half & forth, RING // 2, 0))
    minus = jnp.where(offset > RING // 2, RING - offset, jnp.where(half & jnp.logical_not(forth), RING // 2, 0))
    return (plus, minus), other, offset


def partners(axis, stride, count):
    index = lax.axis_index(axis)
    digit = lax.rem(index // stride, count)
    return [{axis: index + (lax.rem(digit + step, count) - digit) * stride} for step in range(1, count)]


def agree(routes_b, routes_f, plan, tier, held, send, recv):
    me = lax.axis_index("expert")
    z, x = lax.rem(me, RING), me // RING
    groups = [partners(*group) for group in GROUPS]
    barrier = pltpu.get_barrier_semaphore()
    for group in groups:
        for peer in group:
            pl.semaphore_signal(barrier, inc=1, device_id=peer, device_id_type=MESH)

    row = iota((8, 1), 0)
    cap = [jnp.zeros((8, 1), F32), jnp.zeros((8, 1), F32)]
    for hop in range(4):
        for i in range(1):
            cap[i] = jnp.where(jnp.bitwise_and(row, 3) == hop, float(TIERS[i][hop]), cap[i])
    need = jnp.zeros((1, 1), F32)
    ways = []
    for routes in (routes_b, routes_f):
        places = [place_of(routes[k : k + 1, :], z, x) for k in range(2)]
        base = [jnp.zeros((1, TOK), jnp.int32)] * 2
        for offset, _ in places:
            base[0] = jnp.maximum(base[0], jnp.where(offset < 4, offset, 0))
            base[1] = jnp.maximum(base[1], jnp.where(offset > 4, RING - offset, 0))
        best = None
        for option in range(4):
            forths, far = [], list(base)
            for k in range(2):
                offset, other = places[k]
                beside = places[1 - k][0]
                free = jnp.where(other == 0, option % 2, option // 2)
                forth = jnp.where((beside > 0) & (beside < 4), 1, jnp.where(beside > 4, 0, free))
                far[0] = jnp.where((offset == 4) & (forth == 1), 4, far[0])
                far[1] = jnp.where((offset == 4) & (forth == 0), 4, far[1])
                forths.append(forth)
            reach = jnp.where(iota((8, TOK), 0) < 4, far[0], far[1])
            goes = jnp.where(reach > jnp.bitwise_and(iota((8, TOK), 0), 3), 1.0, 0.0)
            count = jnp.sum(goes, axis=1, keepdims=True)
            over = [jnp.sum(jnp.maximum(count - c, 0.0), axis=0, keepdims=True) for c in cap]
            score = over[1] * 65536.0 + over[0] * 1024.0 + jnp.sum(count, axis=0, keepdims=True)
            if best is None:
                best = (score, over, forths)
            else:
                take = score < best[0]
                best = (
                    jnp.where(take, score, best[0]),
                    [jnp.where(take, new, old) for new, old in zip(over, best[1])],
                    [jnp.where(take, new, old) for new, old in zip(forths, best[2])],
                )
        own = jnp.where(best[1][0] > 0, 1.0, 0.0)
        need = jnp.maximum(need, own)
        ways += best[2]
    rows = iota((8, TOK), 0)
    table = jnp.zeros((8, TOK), jnp.int32)
    for i, way in enumerate(ways):
        table = jnp.where(rows == i, way, table)
    plan[...] = table

    pl.semaphore_wait(barrier, sum(len(group) for group in groups))
    total = jnp.broadcast_to(need, (8, TOK))
    for i, group in enumerate(groups):
        held[i, 0] = total
        copies = [
            pltpu.make_async_remote_copy(
                src_ref=held.at[i, 0], dst_ref=held.at[i, step + 1], send_sem=send.at[i, step],
                recv_sem=recv.at[i, step], device_id=peer, device_id_type=MESH,
            )
            for step, peer in enumerate(group)
        ]
        for copy in copies:
            copy.start()
        for step, copy in enumerate(copies):
            copy.wait_recv()
            total = jnp.maximum(total, held[i, step + 1])
        for copy in copies:
            copy.wait_send()
    tier[...] = total.astype(jnp.int32)


def code_of(hop, other):
    return jnp.where(hop > 0, 2 * (hop - 1) + other, -1)


def selector(meta, row):
    slot = iota((SLOTS, TOK), 0).astype(F32) + 1.0
    own = jnp.where(slot == meta[row : row + 1, :], 1.0, 0.0)
    other = jnp.where(slot == meta[row + 1 : row + 2, :], 1.0, 0.0)
    return own, other


def spreader(meta, row):
    own, other = selector(meta, row)
    w_own, w_other = meta[row + 2 : row + 3, :], meta[row + 3 : row + 4, :]
    hi_own, hi_other = w_own.astype(BF16).astype(F32), w_other.astype(BF16).astype(F32)
    stacked = jnp.concatenate(
        [own * hi_own, other * hi_other, own * (w_own - hi_own), other * (w_other - hi_other)], axis=0
    )
    return jnp.transpose(stacked).astype(BF16)


def kernel(
    reach, general, plan_ref, tokens_f_hbm, routes_f, weights_f, tokens_b_hbm, routes_b, weights_b, grads_hbm, gain,
    gate_hbm, up_hbm, down_hbm,
    next_input, next_grad, combine,
    tokens_f, tokens_b, grads, packed, r1, r2, r3, r4, meta0, meta1, meta2, meta3, meta4, meta_here, back,
    xsend, xin, w_gate, w_up, w_down, hid_a, hid_b, y_b, y_f, yx_b, yx_f,
    t1, t2, t3, t4, ct_out, ct_in, res, done_f, done_b,
    d_send, d_recv, m_send, m_recv, x_send, x_recv, y_send, y_recv, t_send, t_recv, c_send, c_recv, s_send, s_recv, w_sem,
):
    me = lax.axis_index("expert")
    z, x = lax.rem(me, RING), me // RING
    seg = lax.axis_index("segment")
    sections = lax.axis_size("segment")
    ahead = {"expert": x * RING + lax.rem(z + 1, RING)}
    behind = {"expert": x * RING + lax.rem(z + RING - 1, RING)}
    across = {"expert": (1 - x) * RING + z}
    seg_next = {"segment": lax.rem(seg + 1, sections)}
    seg_prev = {"segment": lax.rem(seg + sections - 1, sections)}
    onward, homeward = (ahead, behind), (behind, ahead)
    width = tokens_f.shape[1]
    hidden = w_gate.shape[1]
    tile = 512
    tiles = width // tile

    loads = [
        pltpu.make_async_copy(src, dst, w_sem.at[i])
        for i, (src, dst) in enumerate(
            (
                (grads_hbm, grads), (tokens_b_hbm, tokens_b), (tokens_f_hbm, tokens_f),
                (gate_hbm, w_gate), (up_hbm, w_up), (down_hbm, w_down),
            )
        )
    ]
    for load in loads:
        load.start()
    barrier = pltpu.get_barrier_semaphore()
    for device in (ahead, behind, across, seg_next, seg_prev):
        pl.semaphore_signal(barrier, inc=1, device_id=device, device_id_type=MESH)

    def over_tiles(body, size=tile):
        @pl.loop(0, width // size)
        def _(i):
            body(pl.ds(pl.multiple_of(i * size, size), size))

    landing = {1: r1, 2: r2, 3: r3}
    returning = {1: t1, 2: t2, 3: t3}
    metas = (meta0, meta1, meta2, meta3, meta4)

    def landed(array, way, hop):
        if hop == 4:
            return r4.at[array, pl.ds(way * SLOTS, SLOTS)]
        return landing[hop].at[array, way]

    def returned(array, way, hop):
        if hop == 4:
            return t4.at[array, pl.ds(way * SLOTS, SLOTS)]
        return returning[hop].at[array, way]

    def remote(src, dst, send, recv, device):
        return pltpu.make_async_remote_copy(
            src_ref=src, dst_ref=dst, send_sem=send, recv_sem=recv, device_id=device, device_id_type=MESH
        )

    def dispatch(array, way, hop):
        source = packed.at[array, way] if hop == 1 else landing[hop - 1].at[array, way]
        rows = reach[hop - 1]
        at = (array, way, hop - 1)
        return remote(
            source.at[pl.ds(0, rows)], landed(array, way, hop), d_send.at[at], d_recv.at[at], onward[way]
        )

    def meta_copy(route, way, hop):
        at = (route, way, hop - 1)
        return remote(
            metas[hop - 1].at[route, way], metas[hop].at[route, way], m_send.at[at], m_recv.at[at], onward[way]
        )

    def cross(array, block):
        here = pl.ds(block * SLOTS, SLOTS)
        there = pl.ds((8 + block) * SLOTS, SLOTS)
        at = (array, block)
        return remote(xsend.at[array, here], xin.at[array, there], x_send.at[at], x_recv.at[at], across)

    outs, outs_x = (y_b, y_f), (yx_b, yx_f)

    def cross_back(which, block):
        there = pl.ds(block * SLOTS, SLOTS)
        here = pl.ds((8 + block) * SLOTS, SLOTS)
        at = (which, block)
        return remote(
            outs[which].at[here], outs_x[which].at[there], y_send.at[at], y_recv.at[at], across
        )

    reused = (SAVED, FWD)

    def piece_of(piece):
        return pl.ds(piece * (width // PIECES), width // PIECES)

    def give_back(which, way, hop, piece):
        at = (which, way, hop - 1, piece)
        cols = piece_of(piece)
        return remote(
            landed(reused[which], way, hop).at[:, cols], returned(which, way, hop).at[:, cols],
            t_send.at[at], t_recv.at[at], homeward[way],
        )

    def give_scalars(way, hop):
        at = (way, hop - 1)
        return remote(ct_out.at[at], ct_in.at[at], c_send.at[at], c_recv.at[at], homeward[way])

    lane = iota((TOK, TOK), 1)
    sub = iota((TOK, TOK), 0)

    def columns_of(rows):
        stacked = jnp.zeros((TOK, TOK), F32)
        for k, row in enumerate(rows):
            stacked = jnp.where(sub == k, row.astype(F32), stacked)
        turned = jnp.transpose(stacked)
        return [turned[:, k : k + 1].astype(jnp.int32) for k in range(len(rows))]

    def forths_of(route):
        return [None if general else plan_ref[2 * route + k : 2 * route + k + 1, :] for k in range(2)]

    def route_columns(r_row, f_row):
        if general:
            return columns_of(r_row), f_row
        columns = columns_of(r_row + f_row)
        return columns[:2], columns[2:]

    def plan(route, routes_ref, weights_ref):
        r_row = [routes_ref[k : k + 1, :] for k in range(2)]
        w_row = [weights_ref[k : k + 1, :] for k in range(2)]
        f_row = forths_of(route)
        r_col, f_col = route_columns(r_row, f_row)
        slot_row = []
        for k in range(2):
            earlier = jnp.where((sub < lane) & ((r_col[0] == r_row[k]) | (r_col[1] == r_row[k])), 1.0, 0.0)
            slot_row.append(jnp.sum(earlier, axis=0, keepdims=True) + 1.0)
        info_col = [hops_of(r, f, z, x) for r, f in zip(r_col, f_col)]
        info_row = [hops_of(r, f, z, x) for r, f in zip(r_row, f_row)]
        kind = iota((8, TOK), 0)
        here = jnp.zeros((8, TOK), F32)
        for k in range(2):
            _, other, offset = info_row[k]
            value = jnp.where(kind < 2, slot_row[k], w_row[k])
            here = here + jnp.where((offset == 0) & (jnp.bitwise_and(kind, 1) == other) & (kind < 4), value, 0.0)
        meta_here[route] = here
        j = iota((16, TOK), 0)
        target = 2 * jnp.right_shift(j, 2) + jnp.bitwise_and(j, 1)
        is_slot = jnp.bitwise_and(j, 2) == 0
        orders = []
        for way in range(2):
            far_col = jnp.maximum(info_col[0][0][way], info_col[1][0][way])
            far_row = jnp.maximum(info_row[0][0][way], info_row[1][0][way])
            ahead_of_row = (far_col > far_row) | ((far_col == far_row) & (sub < lane))
            pos_row = jnp.sum(jnp.where(ahead_of_row, 1.0, 0.0), axis=0, keepdims=True)
            ahead_of_col = (far_row > far_col) | ((far_row == far_col) & (lane < sub))
            pos_col = jnp.sum(jnp.where(ahead_of_col, 1.0, 0.0), axis=1, keepdims=True)
            order = jnp.where(sub.astype(F32) == pos_row, 1.0, 0.0).astype(BF16)
            back[route, way] = jnp.where(lane.astype(F32) == pos_col, 1.0, 0.0).astype(BF16)
            meta = jnp.zeros((16, TOK), F32)
            for k in range(2):
                code = code_of(info_row[k][0][way], info_row[k][1])
                meta = meta + jnp.where(code == target, jnp.where(is_slot, slot_row[k], w_row[k]), 0.0)
            high = meta.astype(BF16)
            low = (meta - high.astype(F32)).astype(BF16)
            meta0[route, way] = dot_t(high, order) + dot_t(low, order)
            orders.append(order)
        return orders

    def scale_of(tokens):
        values = tokens[...].astype(F32)
        return lax.rsqrt(jnp.mean(values * values, axis=-1, keepdims=True) + EPS)

    def normalize(tokens, out):
        inv = scale_of(tokens)

        def body(cols):
            out[:, cols] = (tokens[:, cols].astype(F32) * inv * gain[:, cols]).astype(BF16)

        over_tiles(body)

    def pack(array, way, order, rows):
        def body(cols):
            packed[array, way, 0 : reach[0], cols] = dot(order[: reach[0]], rows[:, cols]).astype(BF16)

        over_tiles(body)

    def pick_here(array, route, rows):
        own, other = selector(meta_here.at[route], 0)
        both = jnp.concatenate([own, other], axis=0).astype(BF16)

        def body(cols):
            picked = dot(both, rows[:, cols]).astype(BF16)
            xin[array, 0:SLOTS, cols] = picked[:SLOTS]
            xsend[array, 0:SLOTS, cols] = picked[SLOTS:]

        over_tiles(body)
        cross(array, 0).start()

    def pick(array, route, ways, hop):
        block = block_of(ways[0], hop)
        rows = reach[hop - 1]
        at = pl.ds(block * SLOTS, SLOTS)
        matrices = []
        for way in ways:
            own, other = selector(metas[hop].at[route, way], 4 * (hop - 1))
            matrices.append(jnp.concatenate([own, other], axis=0)[:, :rows].astype(BF16))

        def body(cols):
            picked = sum(dot(m, landed(array, w, hop)[:, cols]) for m, w in zip(matrices, ways)).astype(BF16)
            xin[array, at, cols] = picked[:SLOTS]
            xsend[array, at, cols] = picked[SLOTS:]

        over_tiles(body)
        cross(array, block).start()

    def advance(array, hop, route=None):
        for way in range(2):
            if route is not None:
                meta_copy(route, way, hop).wait_recv()
                if hop < 4:
                    meta_copy(route, way, hop + 1).start()
            dispatch(array, way, hop).wait_recv()
            if hop < 4:
                dispatch(array, way, hop + 1).start()

    def pick_all(array, hop, route):
        if hop == 4:
            pick(array, route, (0, 1), 4)
        else:
            pick(array, route, (0,), hop)
            pick(array, route, (1,), hop)

    def spread(which, route, hop):
        rows = reach[hop - 1]
        further = reach[hop] if hop < 4 else 0
        blocks = [pl.ds(block_of(way, hop) * SLOTS, SLOTS) for way in range(2)]
        matrices = [spreader(metas[hop].at[route, way], 4 * (hop - 1))[:rows] for way in range(2)]
        for piece in range(PIECES):
            cols = piece_of(piece)
            for way, at, matrix in zip(range(2), blocks, matrices):
                own, other = outs[which][at, cols], outs_x[which][at, cols]
                total = dot(matrix, jnp.concatenate([own, other, own, other], axis=0))
                if further:
                    give_back(which, way, hop + 1, piece).wait_recv()
                    came = returned(which, way, hop + 1)[:, cols].astype(F32)
                    if further < rows:
                        came = jnp.concatenate([came, jnp.zeros((rows - further, width // PIECES), F32)], axis=0)
                    total = total + came
                landed(reused[which], way, hop)[:, cols] = total.astype(BF16)
                give_back(which, way, hop, piece).start()
        if which == 0:
            extra = pl.ds(width, TOK)
            for way, at in zip(range(2), blocks):
                own, other = selector(metas[hop].at[route, way], 4 * (hop - 1))
                scalars = scalar_rows(own, other, y_b[at, extra], yx_b[at, extra], hop)
                if hop < 4:
                    give_scalars(way, hop + 1).wait_recv()
                    scalars = scalars + ct_in[way, hop]
                ct_out[way, hop - 1] = scalars
                give_scalars(way, hop).start()

    def scalar_rows(own, other, mine, theirs, hop):
        row = iota((8, TOK), 0)
        first = jnp.sum(own * mine.astype(F32), axis=0, keepdims=True)
        second = jnp.sum(other * theirs.astype(F32), axis=0, keepdims=True)
        return jnp.where(row == 2 * (hop - 1), first, jnp.where(row == 2 * (hop - 1) + 1, second, 0.0))

    def gather_sums(which, route, use):
        matrix = spreader(meta_here.at[route], 0)
        orders = [back[route, way][:, : reach[0]] for way in range(2)]
        at = pl.ds(0, SLOTS)
        for piece in range(PIECES):
            cols = piece_of(piece)
            own, other = outs[which][at, cols], outs_x[which][at, cols]
            total = dot(matrix, jnp.concatenate([own, other, own, other], axis=0))
            for way in range(2):
                give_back(which, way, 1, piece).wait_recv()
                total = total + dot(orders[way], returned(which, way, 1)[:, cols])
            use(piece, cols, total)

    def backward_hidden(first, last):
        @pl.loop(first, last)
        def _(i):
            cols = pl.ds(pl.multiple_of(i * 256, 256), 256)
            gate = dot(xin[SAVED], w_gate[:, cols])
            up = dot(xin[SAVED], w_up[:, cols])
            back_in = dot_t(xin[GRAD], w_down[cols, :])
            sigmoid = jax.nn.sigmoid(gate)
            active = gate * sigmoid
            rounded = (active * up).astype(BF16).astype(F32)
            part = jnp.sum(rounded * back_in, axis=1, keepdims=True)
            hid_a[:, cols] = (back_in * up * sigmoid * (1.0 + gate * (1.0 - sigmoid))).astype(BF16)
            hid_b[:, cols] = (back_in * active).astype(BF16)
            res_part = jnp.broadcast_to(part, (part.shape[0], TOK))

            @pl.when(i == 0)
            def _():
                done_b[...] = res_part

            @pl.when(i > 0)
            def _():
                done_b[...] = done_b[...] + res_part

    def backward_rows():
        y_b[:, width : width + TOK] = done_b[...].astype(BF16)

        def body(cols):
            y_b[:, cols] = (dot_t(hid_a[...], w_gate[cols, :]) + dot_t(hid_b[...], w_up[cols, :])).astype(BF16)

        over_tiles(body)

    def forward_hidden():
        @pl.loop(0, hidden // 256)
        def _(i):
            cols = pl.ds(pl.multiple_of(i * 256, 256), 256)
            gate = dot(xin[FWD], w_gate[:, cols])
            up = dot(xin[FWD], w_up[:, cols])
            hid_a[:, cols] = (gate * jax.nn.sigmoid(gate) * up).astype(BF16)

    def forward_rows():
        def body(cols):
            y_f[:, cols] = dot(hid_a[...], w_down[:, cols]).astype(BF16)

        over_tiles(body)

    def start_cross_back(which, blocks):
        for block in blocks:
            cross_back(which, block).start()

    def wait_cross_back(which, blocks):
        for block in blocks:
            cross_back(which, block).wait_recv()

    orders_b = plan(BWD_ROUTE, routes_b, weights_b)
    loads[0].wait()
    for way in range(2):
        pack(GRAD, way, orders_b[way], grads)
    pl.semaphore_wait(barrier, 5)
    for way in range(2):
        dispatch(GRAD, way, 1).start()
    for way in range(2):
        meta_copy(BWD_ROUTE, way, 1).start()
    loads[1].wait()
    normalize(tokens_b, done_f)
    for way in range(2):
        pack(SAVED, way, orders_b[way], done_f)
        dispatch(SAVED, way, 1).start()
    pick_here(GRAD, BWD_ROUTE, grads)
    pick_here(SAVED, BWD_ROUTE, done_f)

    def prepare_forward():
        orders_f = plan(FWD_ROUTE, routes_f, weights_f)
        loads[2].wait()
        normalize(tokens_f, done_f)
        for way in range(2):
            meta_copy(FWD_ROUTE, way, 1).start()
            pack(FWD, way, orders_f[way], done_f)
        pick_here(FWD, FWD_ROUTE, done_f)

    for hop in range(1, 5):
        advance(GRAD, hop, BWD_ROUTE)
        pick_all(GRAD, hop, BWD_ROUTE)
        advance(SAVED, hop)
        if hop == 3:
            for way in range(2):
                dispatch(FWD, way, 1).start()
        pick_all(SAVED, hop, BWD_ROUTE)
        if hop == 1:
            prepare_forward()

    for load in loads[3:]:
        load.wait()
    for block in range(8):
        cross(SAVED, block).wait_recv()
        cross(GRAD, block).wait_recv()
    steps = hidden // 256
    backward_hidden(0, 1)
    advance(FWD, 1, FWD_ROUTE)
    pick_all(FWD, 1, FWD_ROUTE)
    backward_hidden(1, steps)
    backward_rows()
    start_cross_back(0, (LAST,))
    for hop in range(1, 5):
        for way in range(2):
            dispatch(SAVED, way, hop).wait_send()
    advance(FWD, 2, FWD_ROUTE)
    pick_all(FWD, 2, FWD_ROUTE)
    start_cross_back(0, (3, 6))
    wait_cross_back(0, (LAST,))
    spread(0, BWD_ROUTE, 4)
    advance(FWD, 3, FWD_ROUTE)
    pick_all(FWD, 3, FWD_ROUTE)
    wait_cross_back(0, (3, 6))
    spread(0, BWD_ROUTE, 3)
    advance(FWD, 4, FWD_ROUTE)
    pick_all(FWD, 4, FWD_ROUTE)
    start_cross_back(0, (2, 5))
    for block in range(8):
        cross(FWD, block).wait_recv()
    forward_hidden()
    wait_cross_back(0, (2, 5))
    spread(0, BWD_ROUTE, 2)
    forward_rows()
    start_cross_back(1, (LAST, 3, 6))
    start_cross_back(0, (1, 4, 0))
    start_cross_back(1, (2, 5, 1, 4, 0))
    for hop in range(1, 5):
        for way in range(2):
            dispatch(FWD, way, hop).wait_send()
    wait_cross_back(1, (LAST,))
    spread(1, FWD_ROUTE, 4)
    wait_cross_back(1, (3, 6))
    spread(1, FWD_ROUTE, 3)
    wait_cross_back(0, (1, 4, 0))
    spread(0, BWD_ROUTE, 1)
    wait_cross_back(1, (2, 5))
    spread(1, FWD_ROUTE, 2)

    def finish_backward():
        def keep(piece, cols, total):
            res[:, cols] = total

        gather_sums(0, BWD_ROUTE, keep)
        inv = scale_of(tokens_b)
        scaled = res[...] * gain[...]
        inner = jnp.mean(tokens_b[...].astype(F32) * scaled, axis=-1, keepdims=True)
        cubed = inv * inv * inv * inner

        def body(cols):
            values = tokens_b[:, cols].astype(F32)
            grad = grads[:, cols].astype(F32) + inv * (res[:, cols] * gain[:, cols]) - values * cubed
            packed[0, 0, :, cols] = grad.astype(BF16)

        for way in range(2):
            dispatch(GRAD, way, 1).wait_send()
        over_tiles(body)

    grad_out = remote(packed.at[0, 0], next_grad, s_send.at[0], s_recv.at[0], seg_prev)

    def input_out(piece):
        cols = piece_of(piece)
        at = 1 + piece
        return remote(packed.at[0, 1, :, cols], next_input.at[:, cols], s_send.at[at], s_recv.at[at], seg_next)

    finish_backward()
    grad_out.start()
    wait_cross_back(1, (1, 4, 0))
    spread(1, FWD_ROUTE, 1)

    own, other = selector(meta_here.at[BWD_ROUTE], 0)
    at = pl.ds(0, SLOTS)
    extra = pl.ds(width, TOK)
    local = scalar_rows(own, other, y_b[at, extra], yx_b[at, extra], 1)
    unit = jnp.where(lane == sub, 1.0, 0.0).astype(BF16)
    values = [dot_t(unit, local.astype(BF16))]
    for way in range(2):
        give_scalars(way, 1).wait_recv()
        values.append(dot_t(back[BWD_ROUTE, way], ct_in[way, 0].astype(BF16)))
    column = iota((TOK, 8), 1)
    picked = jnp.zeros((TOK, TOK), F32)
    columns = route_columns([routes_b[k : k + 1, :] for k in range(2)], forths_of(BWD_ROUTE))
    for k in range(2):
        hops, off_column, offset = hops_of(columns[0][k], columns[1][k], z, x)
        codes = [jnp.where(offset == 0, off_column, -1)] + [code_of(hop, off_column) for hop in hops]
        total = sum(jnp.where(code == column, value, 0.0) for code, value in zip(codes, values))
        picked = jnp.where(lane == k, jnp.sum(total, axis=1, keepdims=True), picked)
    combine[...] = jnp.transpose(picked)[:2, :].astype(BF16)

    def finish_forward(piece, cols, total):
        packed[0, 1, :, cols] = (tokens_f[:, cols].astype(F32) + total).astype(BF16)
        input_out(piece).start()

    gather_sums(1, FWD_ROUTE, finish_forward)

    for hop in range(1, 5):
        for way in range(2):
            if hop > 1:
                dispatch(GRAD, way, hop).wait_send()
            for route in range(2):
                meta_copy(route, way, hop).wait_send()
                for piece in range(PIECES):
                    give_back(route, way, hop, piece).wait_send()
            give_scalars(way, hop).wait_send()
    for block in range(8):
        for array in range(3):
            cross(array, block).wait_send()
        for which in range(2):
            cross_back(which, block).wait_send()
    for out in [grad_out] + [input_out(piece) for piece in range(PIECES)]:
        out.wait_send()
        out.wait_recv()


def hand_over(*refs):
    half = len(refs) // 2
    for source, target in zip(refs[:half], refs[half:]):
        target[...] = source[...]


def pass_through(number, rows, width, hidden):
    c1, c2, c3, c4 = TIERS[number]
    every = 16 * SLOTS
    vmem = pl.BlockSpec(memory_space=pltpu.VMEM)
    hbm = pl.BlockSpec(memory_space=pl.ANY)
    dma = pltpu.SemaphoreType.DMA
    meta = pltpu.VMEM((2, 2, 16, TOK), F32)
    return pl.pallas_call(
        functools.partial(kernel, TIERS[number], number == len(TIERS) - 1),
        out_shape=(
            jax.ShapeDtypeStruct((rows, width), BF16),
            jax.ShapeDtypeStruct((rows, width), BF16),
            jax.ShapeDtypeStruct((2, rows), BF16),
        ),
        in_specs=[vmem, hbm, vmem, vmem, hbm, vmem, vmem, hbm, vmem] + [hbm] * 3,
        out_specs=(vmem, vmem, vmem),
        scratch_shapes=[
            pltpu.VMEM((rows, width), BF16),
            pltpu.VMEM((rows, width), BF16),
            pltpu.VMEM((rows, width), BF16),
            pltpu.VMEM((3, 2, rows, width), BF16),
            pltpu.VMEM((3, 2, c1, width), BF16),
            pltpu.VMEM((3, 2, c2, width), BF16),
            pltpu.VMEM((3, 2, c3, width), BF16),
            pltpu.VMEM((3, 2 * c4, width), BF16),
            meta, meta, meta, meta, meta,
            pltpu.VMEM((2, 8, TOK), F32),
            pltpu.VMEM((2, 2, TOK, TOK), BF16),
            pltpu.VMEM((3, every // 2, width), BF16),
            pltpu.VMEM((3, every, width), BF16),
            pltpu.VMEM((width, hidden), BF16),
            pltpu.VMEM((width, hidden), BF16),
            pltpu.VMEM((hidden, width), BF16),
            pltpu.VMEM((every, hidden), BF16),
            pltpu.VMEM((every, hidden), BF16),
            pltpu.VMEM((every, width + TOK), BF16),
            pltpu.VMEM((every, width), BF16),
            pltpu.VMEM((every // 2, width + TOK), BF16),
            pltpu.VMEM((every // 2, width), BF16),
            pltpu.VMEM((2, 2, c1, width), BF16),
            pltpu.VMEM((2, 2, c2, width), BF16),
            pltpu.VMEM((2, 2, c3, width), BF16),
            pltpu.VMEM((2, 2 * c4, width), BF16),
            pltpu.VMEM((2, 4, 8, TOK), F32),
            pltpu.VMEM((2, 4, 8, TOK), F32),
            pltpu.VMEM((rows, width), F32),
            pltpu.VMEM((rows, width), BF16),
            pltpu.VMEM((every, TOK), F32),
            dma((3, 2, 4)), dma((3, 2, 4)),
            dma((2, 2, 4)), dma((2, 2, 4)),
            dma((3, 8)), dma((3, 8)),
            dma((2, 8)), dma((2, 8)),
            dma((2, 2, 4, PIECES)), dma((2, 2, 4, PIECES)),
            dma((2, 4)), dma((2, 4)),
            dma((1 + PIECES,)), dma((1 + PIECES,)),
            dma((6,)),
        ],
        compiler_params=pltpu.CompilerParams(
            collective_id=1 + number, has_side_effects=True, vmem_limit_bytes=60 * 1024 * 1024
        ),
        cost_estimate=pl.CostEstimate(
            flops=2 * every * width * hidden * 8, bytes_accessed=6 * width * hidden, transcendentals=2 * every * hidden
        ),
    )


def step(
    fwd_tokens, fwd_routes, fwd_weights, saved_tokens, bwd_routes, bwd_weights, incoming_grad, norm_gain,
    gate_proj, up_proj, down_proj,
):
    rows, width = fwd_tokens.shape[1:]
    hidden = gate_proj.shape[3]
    vmem = pl.BlockSpec(memory_space=pltpu.VMEM)
    dma = pltpu.SemaphoreType.DMA
    most = max(count for _, _, count in GROUPS)
    routes_f, routes_b = fwd_routes[0].T, bwd_routes[0].T
    table = jax.ShapeDtypeStruct((8, TOK), jnp.int32)
    plan, tier = pl.pallas_call(
        agree,
        out_shape=(table, table),
        in_specs=[vmem, vmem],
        out_specs=(vmem, vmem),
        scratch_shapes=[
            pltpu.VMEM((len(GROUPS), most, 8, TOK), F32),
            dma((len(GROUPS), most)), dma((len(GROUPS), most)),
        ],
        compiler_params=pltpu.CompilerParams(collective_id=0, has_side_effects=True),
    )(routes_b, routes_f)
    outs = lax.switch(
        tier[0, 0],
        [pass_through(number, rows, width, hidden) for number in range(len(TIERS))],
        plan, fwd_tokens[0], routes_f, fwd_weights[0].T, saved_tokens[0], routes_b, bwd_weights[0].T,
        incoming_grad[0], norm_gain, gate_proj[0, 0], up_proj[0, 0], down_proj[0, 0],
    )
    outs = pl.pallas_call(
        hand_over,
        out_shape=tuple(jax.ShapeDtypeStruct(out.shape, out.dtype) for out in outs),
        in_specs=[vmem] * 3,
        out_specs=(vmem,) * 3,
    )(*outs)
    return (outs[0][None], outs[1][None], outs[2].T[None])


def solution(mesh):
    rows = P("segment", "expert", None)
    return jax.shard_map(
        step,
        mesh=mesh,
        in_specs=(rows,) * 7 + (P("segment", None),) + (P("segment", "expert", None, None),) * 3,
        out_specs=(rows, rows, rows),
        check_vma=False,
    )
```

```python
import functools

import jax
import jax.numpy as jnp
from jax import lax
from jax.experimental import pallas as pl
from jax.experimental.pallas import tpu as pltpu
from jax.sharding import PartitionSpec as P

EPS = 1e-06
MESH = pl.DeviceIdType.MESH
F32 = jnp.float32
BF16 = jnp.bfloat16
SLOTS = 32
TOK = 128
RING = 8
TIERS = ((96, 96, 80, SLOTS), (TOK, TOK, 3 * SLOTS, SLOTS))
SAVED, GRAD, FWD = 0, 1, 2
BWD_ROUTE, FWD_ROUTE = 0, 1
PIECES = 4
GROUPS = (("expert", 1, 16), ("segment", 1, 16))
LAST = 7


def block_of(way, hop):
    return LAST if hop == 4 else 3 * way + hop


def iota(shape, dim):
    return lax.broadcasted_iota(jnp.int32, shape, dim)


def dot(a, b):
    return jnp.dot(a, b, preferred_element_type=F32)


def dot_t(a, b):
    return lax.dot_general(a, b, (((1,), (1,)), ((), ())), preferred_element_type=F32)


def place_of(route, z, x):
    offset = jnp.bitwise_and(route - z + RING, RING - 1)
    return offset, jnp.where(jnp.right_shift(route, 3) != x, 1, 0)


def hops_of(route, forth, z, x):
    offset, other = place_of(route, z, x)
    half = offset == RING // 2
    forth = other == 0 if forth is None else forth == 1
    plus = jnp.where(offset < RING // 2, offset, jnp.where(half & forth, RING // 2, 0))
    minus = jnp.where(offset > RING // 2, RING - offset, jnp.where(half & jnp.logical_not(forth), RING // 2, 0))
    return (plus, minus), other, offset


def partners(axis, stride, count):
    index = lax.axis_index(axis)
    digit = lax.rem(index // stride, count)
    return [{axis: index + (lax.rem(digit + step, count) - digit) * stride} for step in range(1, count)]


def agree(routes_b, routes_f, plan, tier, held, send, recv):
    me = lax.axis_index("expert")
    z, x = lax.rem(me, RING), me // RING
    groups = [partners(*group) for group in GROUPS]
    barrier = pltpu.get_barrier_semaphore()
    for group in groups:
        for peer in group:
            pl.semaphore_signal(barrier, inc=1, device_id=peer, device_id_type=MESH)

    row = iota((8, 1), 0)
    cap = [jnp.zeros((8, 1), F32), jnp.zeros((8, 1), F32)]
    for hop in range(4):
        for i in range(1):
            cap[i] = jnp.where(jnp.bitwise_and(row, 3) == hop, float(TIERS[i][hop]), cap[i])
    need = jnp.zeros((1, 1), F32)
    ways = []
    for routes in (routes_b, routes_f):
        places = [place_of(routes[k : k + 1, :], z, x) for k in range(2)]
        base = [jnp.zeros((1, TOK), jnp.int32)] * 2
        for offset, _ in places:
            base[0] = jnp.maximum(base[0], jnp.where(offset < 4, offset, 0))
            base[1] = jnp.maximum(base[1], jnp.where(offset > 4, RING - offset, 0))
        best = None
        for option in range(4):
            forths, far = [], list(base)
            for k in range(2):
                offset, other = places[k]
                beside = places[1 - k][0]
                free = jnp.where(other == 0, option % 2, option // 2)
                forth = jnp.where((beside > 0) & (beside < 4), 1, jnp.where(beside > 4, 0, free))
                far[0] = jnp.where((offset == 4) & (forth == 1), 4, far[0])
                far[1] = jnp.where((offset == 4) & (forth == 0), 4, far[1])
                forths.append(forth)
            reach = jnp.where(iota((8, TOK), 0) < 4, far[0], far[1])
            goes = jnp.where(reach > jnp.bitwise_and(iota((8, TOK), 0), 3), 1.0, 0.0)
            count = jnp.sum(goes, axis=1, keepdims=True)
            over = [jnp.sum(jnp.maximum(count - c, 0.0), axis=0, keepdims=True) for c in cap]
            score = over[1] * 65536.0 + over[0] * 1024.0 + jnp.sum(count, axis=0, keepdims=True)
            if best is None:
                best = (score, over, forths)
            else:
                take = score < best[0]
                best = (
                    jnp.where(take, score, best[0]),
                    [jnp.where(take, new, old) for new, old in zip(over, best[1])],
                    [jnp.where(take, new, old) for new, old in zip(forths, best[2])],
                )
        own = jnp.where(best[1][0] > 0, 1.0, 0.0)
        need = jnp.maximum(need, own)
        ways += best[2]
    rows = iota((8, TOK), 0)
    table = jnp.zeros((8, TOK), jnp.int32)
    for i, way in enumerate(ways):
        table = jnp.where(rows == i, way, table)
    plan[...] = table

    pl.semaphore_wait(barrier, sum(len(group) for group in groups))
    total = jnp.broadcast_to(need, (8, TOK))
    for i, group in enumerate(groups):
        held[i, 0] = total
        copies = [
            pltpu.make_async_remote_copy(
                src_ref=held.at[i, 0], dst_ref=held.at[i, step + 1], send_sem=send.at[i, step],
                recv_sem=recv.at[i, step], device_id=peer, device_id_type=MESH,
            )
            for step, peer in enumerate(group)
        ]
        for copy in copies:
            copy.start()
        for step, copy in enumerate(copies):
            copy.wait_recv()
            total = jnp.maximum(total, held[i, step + 1])
        for copy in copies:
            copy.wait_send()
    tier[...] = total.astype(jnp.int32)


def code_of(hop, other):
    return jnp.where(hop > 0, 2 * (hop - 1) + other, -1)


def selector(meta, row):
    slot = iota((SLOTS, TOK), 0).astype(F32) + 1.0
    own = jnp.where(slot == meta[row : row + 1, :], 1.0, 0.0)
    other = jnp.where(slot == meta[row + 1 : row + 2, :], 1.0, 0.0)
    return own, other


def spreader(meta, row):
    own, other = selector(meta, row)
    w_own, w_other = meta[row + 2 : row + 3, :], meta[row + 3 : row + 4, :]
    hi_own, hi_other = w_own.astype(BF16).astype(F32), w_other.astype(BF16).astype(F32)
    stacked = jnp.concatenate(
        [own * hi_own, other * hi_other, own * (w_own - hi_own), other * (w_other - hi_other)], axis=0
    )
    return jnp.transpose(stacked).astype(BF16)


def kernel(
    reach, general, plan_ref, tokens_f_hbm, routes_f, weights_f, tokens_b_hbm, routes_b, weights_b, grads_hbm, gain,
    gate_hbm, up_hbm, down_hbm,
    next_input, next_grad, combine,
    tokens_f, tokens_b, grads, packed, r1, r2, r3, r4, meta0, meta1, meta2, meta3, meta4, meta_here, back,
    xsend, xin, w_gate, w_up, w_down, hid_a, hid_b, y_b, y_f, yx_b, yx_f,
    t1, t2, t3, t4, ct_out, ct_in, res, done_f, done_b,
    d_send, d_recv, m_send, m_recv, x_send, x_recv, y_send, y_recv, t_send, t_recv, c_send, c_recv, s_send, s_recv, w_sem,
):
    me = lax.axis_index("expert")
    z, x = lax.rem(me, RING), me // RING
    seg = lax.axis_index("segment")
    sections = lax.axis_size("segment")
    ahead = {"expert": x * RING + lax.rem(z + 1, RING)}
    behind = {"expert": x * RING + lax.rem(z + RING - 1, RING)}
    across = {"expert": (1 - x) * RING + z}
    seg_next = {"segment": lax.rem(seg + 1, sections)}
    seg_prev = {"segment": lax.rem(seg + sections - 1, sections)}
    onward, homeward = (ahead, behind), (behind, ahead)
    width = tokens_f.shape[1]
    hidden = w_gate.shape[1]
    tile = 512
    tiles = width // tile

    loads = [
        pltpu.make_async_copy(src, dst, w_sem.at[i])
        for i, (src, dst) in enumerate(
            (
                (grads_hbm, grads), (tokens_b_hbm, tokens_b), (tokens_f_hbm, tokens_f),
                (gate_hbm, w_gate), (up_hbm, w_up), (down_hbm, w_down),
            )
        )
    ]
    for load in loads:
        load.start()
    barrier = pltpu.get_barrier_semaphore()
    for device in (ahead, behind, across, seg_next, seg_prev):
        pl.semaphore_signal(barrier, inc=1, device_id=device, device_id_type=MESH)

    def over_tiles(body, size=tile):
        @pl.loop(0, width // size)
        def _(i):
            body(pl.ds(pl.multiple_of(i * size, size), size))

    landing = {1: r1, 2: r2, 3: r3}
    returning = {1: t1, 2: t2, 3: t3}
    metas = (meta0, meta1, meta2, meta3, meta4)

    def landed(array, way, hop):
        if hop == 4:
            return r4.at[array, pl.ds(way * SLOTS, SLOTS)]
        return landing[hop].at[array, way]

    def returned(array, way, hop):
        if hop == 4:
            return t4.at[array, pl.ds(way * SLOTS, SLOTS)]
        return returning[hop].at[array, way]

    def remote(src, dst, send, recv, device):
        return pltpu.make_async_remote_copy(
            src_ref=src, dst_ref=dst, send_sem=send, recv_sem=recv, device_id=device, device_id_type=MESH
        )

    def dispatch(array, way, hop):
        source = packed.at[array, way] if hop == 1 else landing[hop - 1].at[array, way]
        rows = reach[hop - 1]
        at = (array, way, hop - 1)
        return remote(
            source.at[pl.ds(0, rows)], landed(array, way, hop), d_send.at[at], d_recv.at[at], onward[way]
        )

    def meta_copy(route, way, hop):
        at = (route, way, hop - 1)
        return remote(
            metas[hop - 1].at[route, way], metas[hop].at[route, way], m_send.at[at], m_recv.at[at], onward[way]
        )

    def cross(array, block):
        here = pl.ds(block * SLOTS, SLOTS)
        there = pl.ds((8 + block) * SLOTS, SLOTS)
        at = (array, block)
        return remote(xsend.at[array, here], xin.at[array, there], x_send.at[at], x_recv.at[at], across)

    outs, outs_x = (y_b, y_f), (yx_b, yx_f)

    def cross_back(which, block):
        there = pl.ds(block * SLOTS, SLOTS)
        here = pl.ds((8 + block) * SLOTS, SLOTS)
        at = (which, block)
        return remote(
            outs[which].at[here], outs_x[which].at[there], y_send.at[at], y_recv.at[at], across
        )

    reused = (SAVED, FWD)

    def piece_of(piece):
        return pl.ds(piece * (width // PIECES), width // PIECES)

    def give_back(which, way, hop, piece):
        at = (which, way, hop - 1, piece)
        cols = piece_of(piece)
        return remote(
            landed(reused[which], way, hop).at[:, cols], returned(which, way, hop).at[:, cols],
            t_send.at[at], t_recv.at[at], homeward[way],
        )

    def give_scalars(way, hop):
        at = (way, hop - 1)
        return remote(ct_out.at[at], ct_in.at[at], c_send.at[at], c_recv.at[at], homeward[way])

    lane = iota((TOK, TOK), 1)
    sub = iota((TOK, TOK), 0)

    def columns_of(rows):
        stacked = jnp.zeros((TOK, TOK), F32)
        for k, row in enumerate(rows):
            stacked = jnp.where(sub == k, row.astype(F32), stacked)
        turned = jnp.transpose(stacked)
        return [turned[:, k : k + 1].astype(jnp.int32) for k in range(len(rows))]

    def forths_of(route):
        return [None if general else plan_ref[2 * route + k : 2 * route + k + 1, :] for k in range(2)]

    def route_columns(r_row, f_row):
        if general:
            return columns_of(r_row), f_row
        columns = columns_of(r_row + f_row)
        return columns[:2], columns[2:]

    def plan(route, routes_ref, weights_ref):
        r_row = [routes_ref[k : k + 1, :] for k in range(2)]
        w_row = [weights_ref[k : k + 1, :] for k in range(2)]
        f_row = forths_of(route)
        r_col, f_col = route_columns(r_row, f_row)
        slot_row = []
        for k in range(2):
            earlier = jnp.where((sub < lane) & ((r_col[0] == r_row[k]) | (r_col[1] == r_row[k])), 1.0, 0.0)
            slot_row.append(jnp.sum(earlier, axis=0, keepdims=True) + 1.0)
        info_col = [hops_of(r, f, z, x) for r, f in zip(r_col, f_col)]
        info_row = [hops_of(r, f, z, x) for r, f in zip(r_row, f_row)]
        kind = iota((8, TOK), 0)
        here = jnp.zeros((8, TOK), F32)
        for k in range(2):
            _, other, offset = info_row[k]
            value = jnp.where(kind < 2, slot_row[k], w_row[k])
            here = here + jnp.where((offset == 0) & (jnp.bitwise_and(kind, 1) == other) & (kind < 4), value, 0.0)
        meta_here[route] = here
        j = iota((16, TOK), 0)
        target = 2 * jnp.right_shift(j, 2) + jnp.bitwise_and(j, 1)
        is_slot = jnp.bitwise_and(j, 2) == 0
        orders = []
        for way in range(2):
            far_col = jnp.maximum(info_col[0][0][way], info_col[1][0][way])
            far_row = jnp.maximum(info_row[0][0][way], info_row[1][0][way])
            ahead_of_row = (far_col > far_row) | ((far_col == far_row) & (sub < lane))
            pos_row = jnp.sum(jnp.where(ahead_of_row, 1.0, 0.0), axis=0, keepdims=True)
            ahead_of_col = (far_row > far_col) | ((far_row == far_col) & (lane < sub))
            pos_col = jnp.sum(jnp.where(ahead_of_col, 1.0, 0.0), axis=1, keepdims=True)
            order = jnp.where(sub.astype(F32) == pos_row, 1.0, 0.0).astype(BF16)
            back[route, way] = jnp.where(lane.astype(F32) == pos_col, 1.0, 0.0).astype(BF16)
            meta = jnp.zeros((16, TOK), F32)
            for k in range(2):
                code = code_of(info_row[k][0][way], info_row[k][1])
                meta = meta + jnp.where(code == target, jnp.where(is_slot, slot_row[k], w_row[k]), 0.0)
            high = meta.astype(BF16)
            low = (meta - high.astype(F32)).astype(BF16)
            meta0[route, way] = dot_t(high, order) + dot_t(low, order)
            orders.append(order)
        return orders

    def scale_of(tokens):
        values = tokens[...].astype(F32)
        return lax.rsqrt(jnp.mean(values * values, axis=-1, keepdims=True) + EPS)

    def normalize(tokens, out):
        inv = scale_of(tokens)

        def body(cols):
            out[:, cols] = (tokens[:, cols].astype(F32) * inv * gain[:, cols]).astype(BF16)

        over_tiles(body)

    def pack(array, way, order, rows):
        def body(cols):
            packed[array, way, 0 : reach[0], cols] = dot(order[: reach[0]], rows[:, cols]).astype(BF16)

        over_tiles(body)

    def pick_here(array, route, rows):
        own, other = selector(meta_here.at[route], 0)
        both = jnp.concatenate([own, other], axis=0).astype(BF16)

        def body(cols):
            picked = dot(both, rows[:, cols]).astype(BF16)
            xin[array, 0:SLOTS, cols] = picked[:SLOTS]
            xsend[array, 0:SLOTS, cols] = picked[SLOTS:]

        over_tiles(body)
        cross(array, 0).start()

    def pick(array, route, ways, hop):
        block = block_of(ways[0], hop)
        rows = reach[hop - 1]
        at = pl.ds(block * SLOTS, SLOTS)
        matrices = []
        for way in ways:
            own, other = selector(metas[hop].at[route, way], 4 * (hop - 1))
            matrices.append(jnp.concatenate([own, other], axis=0)[:, :rows].astype(BF16))

        def body(cols):
            picked = sum(dot(m, landed(array, w, hop)[:, cols]) for m, w in zip(matrices, ways)).astype(BF16)
            xin[array, at, cols] = picked[:SLOTS]
            xsend[array, at, cols] = picked[SLOTS:]

        over_tiles(body)
        cross(array, block).start()

    def advance(array, hop, route=None):
        for way in range(2):
            if route is not None:
                meta_copy(route, way, hop).wait_recv()
                if hop < 4:
                    meta_copy(route, way, hop + 1).start()
            dispatch(array, way, hop).wait_recv()
            if hop < 4:
                dispatch(array, way, hop + 1).start()

    def pick_all(array, hop, route):
        if hop == 4:
            pick(array, route, (0, 1), 4)
        else:
            pick(array, route, (0,), hop)
            pick(array, route, (1,), hop)

    def spread(which, route, hop):
        rows = reach[hop - 1]
        further = reach[hop] if hop < 4 else 0
        blocks = [pl.ds(block_of(way, hop) * SLOTS, SLOTS) for way in range(2)]
        matrices = [spreader(metas[hop].at[route, way], 4 * (hop - 1))[:rows] for way in range(2)]
        for piece in range(PIECES):
            cols = piece_of(piece)
            for way, at, matrix in zip(range(2), blocks, matrices):
                own, other = outs[which][at, cols], outs_x[which][at, cols]
                total = dot(matrix, jnp.concatenate([own, other, own, other], axis=0))
                if further:
                    give_back(which, way, hop + 1, piece).wait_recv()
                    came = returned(which, way, hop + 1)[:, cols].astype(F32)
                    if further < rows:
                        came = jnp.concatenate([came, jnp.zeros((rows - further, width // PIECES), F32)], axis=0)
                    total = total + came
                landed(reused[which], way, hop)[:, cols] = total.astype(BF16)
                give_back(which, way, hop, piece).start()
        if which == 0:
            extra = pl.ds(width, TOK)
            for way, at in zip(range(2), blocks):
                own, other = selector(metas[hop].at[route, way], 4 * (hop - 1))
                scalars = scalar_rows(own, other, y_b[at, extra], yx_b[at, extra], hop)
                if hop < 4:
                    give_scalars(way, hop + 1).wait_recv()
                    scalars = scalars + ct_in[way, hop]
                ct_out[way, hop - 1] = scalars
                give_scalars(way, hop).start()

    def scalar_rows(own, other, mine, theirs, hop):
        row = iota((8, TOK), 0)
        first = jnp.sum(own * mine.astype(F32), axis=0, keepdims=True)
        second = jnp.sum(other * theirs.astype(F32), axis=0, keepdims=True)
        return jnp.where(row == 2 * (hop - 1), first, jnp.where(row == 2 * (hop - 1) + 1, second, 0.0))

    def gather_sums(which, route, use):
        matrix = spreader(meta_here.at[route], 0)
        orders = [back[route, way][:, : reach[0]] for way in range(2)]
        at = pl.ds(0, SLOTS)
        for piece in range(PIECES):
            cols = piece_of(piece)
            own, other = outs[which][at, cols], outs_x[which][at, cols]
            total = dot(matrix, jnp.concatenate([own, other, own, other], axis=0))
            for way in range(2):
                give_back(which, way, 1, piece).wait_recv()
                total = total + dot(orders[way], returned(which, way, 1)[:, cols])
            use(piece, cols, total)

    half_rows = 8 * SLOTS

    def backward_hidden(half, first, last):
        at = pl.ds(half * half_rows, half_rows)

        @pl.loop(first, last)
        def _(i):
            cols = pl.ds(pl.multiple_of(i * 256, 256), 256)
            gate = dot(xin[SAVED, at], w_gate[:, cols])
            up = dot(xin[SAVED, at], w_up[:, cols])
            back_in = dot_t(xin[GRAD, at], w_down[cols, :])
            sigmoid = jax.nn.sigmoid(gate)
            active = gate * sigmoid
            rounded = (active * up).astype(BF16).astype(F32)
            part = jnp.sum(rounded * back_in, axis=1, keepdims=True)
            hid_a[at, cols] = (back_in * up * sigmoid * (1.0 + gate * (1.0 - sigmoid))).astype(BF16)
            hid_b[at, cols] = (back_in * active).astype(BF16)
            res_part = jnp.broadcast_to(part, (part.shape[0], TOK))

            @pl.when(i == 0)
            def _():
                done_b[at, :] = res_part

            @pl.when(i > 0)
            def _():
                done_b[at, :] = done_b[at, :] + res_part

    def backward_rows():
        y_b[:, width : width + TOK] = done_b[...].astype(BF16)

        def body(cols):
            y_b[:, cols] = (dot_t(hid_a[...], w_gate[cols, :]) + dot_t(hid_b[...], w_up[cols, :])).astype(BF16)

        over_tiles(body)

    def forward_hidden():
        @pl.loop(0, hidden // 256)
        def _(i):
            cols = pl.ds(pl.multiple_of(i * 256, 256), 256)
            gate = dot(xin[FWD], w_gate[:, cols])
            up = dot(xin[FWD], w_up[:, cols])
            hid_a[:, cols] = (gate * jax.nn.sigmoid(gate) * up).astype(BF16)

    def forward_rows():
        def body(cols):
            y_f[:, cols] = dot(hid_a[...], w_down[:, cols]).astype(BF16)

        over_tiles(body)

    def start_cross_back(which, blocks):
        for block in blocks:
            cross_back(which, block).start()

    def wait_cross_back(which, blocks):
        for block in blocks:
            cross_back(which, block).wait_recv()

    orders_b = plan(BWD_ROUTE, routes_b, weights_b)
    loads[0].wait()
    for way in range(2):
        pack(GRAD, way, orders_b[way], grads)
    pl.semaphore_wait(barrier, 5)
    for way in range(2):
        dispatch(GRAD, way, 1).start()
    for way in range(2):
        meta_copy(BWD_ROUTE, way, 1).start()
    loads[1].wait()
    normalize(tokens_b, done_f)
    for way in range(2):
        pack(SAVED, way, orders_b[way], done_f)
        dispatch(SAVED, way, 1).start()
    pick_here(GRAD, BWD_ROUTE, grads)
    pick_here(SAVED, BWD_ROUTE, done_f)

    def prepare_forward():
        orders_f = plan(FWD_ROUTE, routes_f, weights_f)
        loads[2].wait()
        normalize(tokens_f, done_f)
        for way in range(2):
            meta_copy(FWD_ROUTE, way, 1).start()
            pack(FWD, way, orders_f[way], done_f)
        pick_here(FWD, FWD_ROUTE, done_f)

    for hop in range(1, 5):
        advance(GRAD, hop, BWD_ROUTE)
        pick_all(GRAD, hop, BWD_ROUTE)
        advance(SAVED, hop)
        if hop == 3:
            for way in range(2):
                dispatch(FWD, way, 1).start()
        pick_all(SAVED, hop, BWD_ROUTE)
        if hop == 1:
            prepare_forward()

    for load in loads[3:]:
        load.wait()
    steps = hidden // 256
    backward_hidden(0, 0, steps)
    for block in range(8):
        cross(SAVED, block).wait_recv()
        cross(GRAD, block).wait_recv()
    advance(FWD, 1, FWD_ROUTE)
    pick_all(FWD, 1, FWD_ROUTE)
    backward_hidden(1, 0, steps)
    backward_rows()
    start_cross_back(0, (LAST,))
    for hop in range(1, 5):
        for way in range(2):
            dispatch(SAVED, way, hop).wait_send()
    advance(FWD, 2, FWD_ROUTE)
    pick_all(FWD, 2, FWD_ROUTE)
    start_cross_back(0, (3, 6))
    wait_cross_back(0, (LAST,))
    spread(0, BWD_ROUTE, 4)
    advance(FWD, 3, FWD_ROUTE)
    pick_all(FWD, 3, FWD_ROUTE)
    wait_cross_back(0, (3, 6))
    spread(0, BWD_ROUTE, 3)
    advance(FWD, 4, FWD_ROUTE)
    pick_all(FWD, 4, FWD_ROUTE)
    start_cross_back(0, (2, 5))
    for block in range(8):
        cross(FWD, block).wait_recv()
    forward_hidden()
    wait_cross_back(0, (2, 5))
    spread(0, BWD_ROUTE, 2)
    forward_rows()
    start_cross_back(1, (LAST, 3, 6))
    start_cross_back(0, (1, 4, 0))
    start_cross_back(1, (2, 5, 1, 4, 0))
    for hop in range(1, 5):
        for way in range(2):
            dispatch(FWD, way, hop).wait_send()
    wait_cross_back(1, (LAST,))
    spread(1, FWD_ROUTE, 4)
    wait_cross_back(1, (3, 6))
    spread(1, FWD_ROUTE, 3)
    wait_cross_back(0, (1, 4, 0))
    spread(0, BWD_ROUTE, 1)
    wait_cross_back(1, (2, 5))
    spread(1, FWD_ROUTE, 2)

    def finish_backward():
        def keep(piece, cols, total):
            res[:, cols] = total

        gather_sums(0, BWD_ROUTE, keep)
        inv = scale_of(tokens_b)
        scaled = res[...] * gain[...]
        inner = jnp.mean(tokens_b[...].astype(F32) * scaled, axis=-1, keepdims=True)
        cubed = inv * inv * inv * inner

        def body(cols):
            values = tokens_b[:, cols].astype(F32)
            grad = grads[:, cols].astype(F32) + inv * (res[:, cols] * gain[:, cols]) - values * cubed
            packed[0, 0, :, cols] = grad.astype(BF16)

        for way in range(2):
            dispatch(GRAD, way, 1).wait_send()
        over_tiles(body)

    grad_out = remote(packed.at[0, 0], next_grad, s_send.at[0], s_recv.at[0], seg_prev)

    def input_out(piece):
        cols = piece_of(piece)
        at = 1 + piece
        return remote(packed.at[0, 1, :, cols], next_input.at[:, cols], s_send.at[at], s_recv.at[at], seg_next)

    finish_backward()
    grad_out.start()
    wait_cross_back(1, (1, 4, 0))
    spread(1, FWD_ROUTE, 1)

    own, other = selector(meta_here.at[BWD_ROUTE], 0)
    at = pl.ds(0, SLOTS)
    extra = pl.ds(width, TOK)
    local = scalar_rows(own, other, y_b[at, extra], yx_b[at, extra], 1)
    unit = jnp.where(lane == sub, 1.0, 0.0).astype(BF16)
    values = [dot_t(unit, local.astype(BF16))]
    for way in range(2):
        give_scalars(way, 1).wait_recv()
        values.append(dot_t(back[BWD_ROUTE, way], ct_in[way, 0].astype(BF16)))
    column = iota((TOK, 8), 1)
    picked = jnp.zeros((TOK, TOK), F32)
    columns = route_columns([routes_b[k : k + 1, :] for k in range(2)], forths_of(BWD_ROUTE))
    for k in range(2):
        hops, off_column, offset = hops_of(columns[0][k], columns[1][k], z, x)
        codes = [jnp.where(offset == 0, off_column, -1)] + [code_of(hop, off_column) for hop in hops]
        total = sum(jnp.where(code == column, value, 0.0) for code, value in zip(codes, values))
        picked = jnp.where(lane == k, jnp.sum(total, axis=1, keepdims=True), picked)
    combine[...] = jnp.transpose(picked)[:2, :].astype(BF16)

    def finish_forward(piece, cols, total):
        packed[0, 1, :, cols] = (tokens_f[:, cols].astype(F32) + total).astype(BF16)
        input_out(piece).start()

    gather_sums(1, FWD_ROUTE, finish_forward)

    for hop in range(1, 5):
        for way in range(2):
            if hop > 1:
                dispatch(GRAD, way, hop).wait_send()
            for route in range(2):
                meta_copy(route, way, hop).wait_send()
                for piece in range(PIECES):
                    give_back(route, way, hop, piece).wait_send()
            give_scalars(way, hop).wait_send()
    for block in range(8):
        for array in range(3):
            cross(array, block).wait_send()
        for which in range(2):
            cross_back(which, block).wait_send()
    for out in [grad_out] + [input_out(piece) for piece in range(PIECES)]:
        out.wait_send()
        out.wait_recv()


def hand_over(*refs):
    half = len(refs) // 2
    for source, target in zip(refs[:half], refs[half:]):
        target[...] = source[...]


def pass_through(number, rows, width, hidden):
    c1, c2, c3, c4 = TIERS[number]
    every = 16 * SLOTS
    vmem = pl.BlockSpec(memory_space=pltpu.VMEM)
    hbm = pl.BlockSpec(memory_space=pl.ANY)
    dma = pltpu.SemaphoreType.DMA
    meta = pltpu.VMEM((2, 2, 16, TOK), F32)
    return pl.pallas_call(
        functools.partial(kernel, TIERS[number], number == len(TIERS) - 1),
        out_shape=(
            jax.ShapeDtypeStruct((rows, width), BF16),
            jax.ShapeDtypeStruct((rows, width), BF16),
            jax.ShapeDtypeStruct((2, rows), BF16),
        ),
        in_specs=[vmem, hbm, vmem, vmem, hbm, vmem, vmem, hbm, vmem] + [hbm] * 3,
        out_specs=(vmem, vmem, vmem),
        scratch_shapes=[
            pltpu.VMEM((rows, width), BF16),
            pltpu.VMEM((rows, width), BF16),
            pltpu.VMEM((rows, width), BF16),
            pltpu.VMEM((3, 2, rows, width), BF16),
            pltpu.VMEM((3, 2, c1, width), BF16),
            pltpu.VMEM((3, 2, c2, width), BF16),
            pltpu.VMEM((3, 2, c3, width), BF16),
            pltpu.VMEM((3, 2 * c4, width), BF16),
            meta, meta, meta, meta, meta,
            pltpu.VMEM((2, 8, TOK), F32),
            pltpu.VMEM((2, 2, TOK, TOK), BF16),
            pltpu.VMEM((3, every // 2, width), BF16),
            pltpu.VMEM((3, every, width), BF16),
            pltpu.VMEM((width, hidden), BF16),
            pltpu.VMEM((width, hidden), BF16),
            pltpu.VMEM((hidden, width), BF16),
            pltpu.VMEM((every, hidden), BF16),
            pltpu.VMEM((every, hidden), BF16),
            pltpu.VMEM((every, width + TOK), BF16),
            pltpu.VMEM((every, width), BF16),
            pltpu.VMEM((every // 2, width + TOK), BF16),
            pltpu.VMEM((every // 2, width), BF16),
            pltpu.VMEM((2, 2, c1, width), BF16),
            pltpu.VMEM((2, 2, c2, width), BF16),
            pltpu.VMEM((2, 2, c3, width), BF16),
            pltpu.VMEM((2, 2 * c4, width), BF16),
            pltpu.VMEM((2, 4, 8, TOK), F32),
            pltpu.VMEM((2, 4, 8, TOK), F32),
            pltpu.VMEM((rows, width), F32),
            pltpu.VMEM((rows, width), BF16),
            pltpu.VMEM((every, TOK), F32),
            dma((3, 2, 4)), dma((3, 2, 4)),
            dma((2, 2, 4)), dma((2, 2, 4)),
            dma((3, 8)), dma((3, 8)),
            dma((2, 8)), dma((2, 8)),
            dma((2, 2, 4, PIECES)), dma((2, 2, 4, PIECES)),
            dma((2, 4)), dma((2, 4)),
            dma((1 + PIECES,)), dma((1 + PIECES,)),
            dma((6,)),
        ],
        compiler_params=pltpu.CompilerParams(
            collective_id=1 + number, has_side_effects=True, vmem_limit_bytes=60 * 1024 * 1024
        ),
        cost_estimate=pl.CostEstimate(
            flops=2 * every * width * hidden * 8, bytes_accessed=6 * width * hidden, transcendentals=2 * every * hidden
        ),
    )


def step(
    fwd_tokens, fwd_routes, fwd_weights, saved_tokens, bwd_routes, bwd_weights, incoming_grad, norm_gain,
    gate_proj, up_proj, down_proj,
):
    rows, width = fwd_tokens.shape[1:]
    hidden = gate_proj.shape[3]
    vmem = pl.BlockSpec(memory_space=pltpu.VMEM)
    dma = pltpu.SemaphoreType.DMA
    most = max(count for _, _, count in GROUPS)
    routes_f, routes_b = fwd_routes[0].T, bwd_routes[0].T
    table = jax.ShapeDtypeStruct((8, TOK), jnp.int32)
    plan, tier = pl.pallas_call(
        agree,
        out_shape=(table, table),
        in_specs=[vmem, vmem],
        out_specs=(vmem, vmem),
        scratch_shapes=[
            pltpu.VMEM((len(GROUPS), most, 8, TOK), F32),
            dma((len(GROUPS), most)), dma((len(GROUPS), most)),
        ],
        compiler_params=pltpu.CompilerParams(collective_id=0, has_side_effects=True),
    )(routes_b, routes_f)
    outs = lax.switch(
        tier[0, 0],
        [pass_through(number, rows, width, hidden) for number in range(len(TIERS))],
        plan, fwd_tokens[0], routes_f, fwd_weights[0].T, saved_tokens[0], routes_b, bwd_weights[0].T,
        incoming_grad[0], norm_gain, gate_proj[0, 0], up_proj[0, 0], down_proj[0, 0],
    )
    outs = pl.pallas_call(
        hand_over,
        out_shape=tuple(jax.ShapeDtypeStruct(out.shape, out.dtype) for out in outs),
        in_specs=[vmem] * 3,
        out_specs=(vmem,) * 3,
    )(*outs)
    return (outs[0][None], outs[1][None], outs[2].T[None])


def solution(mesh):
    rows = P("segment", "expert", None)
    return jax.shard_map(
        step,
        mesh=mesh,
        in_specs=(rows,) * 7 + (P("segment", None),) + (P("segment", "expert", None, None),) * 3,
        out_specs=(rows, rows, rows),
        check_vma=False,
    )
```
